32 devices in a mesh: grp: 2 (over y), seg: 8 (over z, x), yoke: 2 (over core).
Axes of the slice: x: 2, y: 2, z: 4, core: 2. Of those that a mesh axis runs over, the one named last changes fastest.
Arguments:
- seg_mid: float32 [3, 4096], P(None, ('grp', 'seg')), parts along dimension 1, may hold values from -1 to 1
- seg_vec: float32 [3, 4096], P(None, ('grp', 'seg')), parts along dimension 1, may hold values from -6 to 6
- strand_of: int32 [4096], P(('grp', 'seg')), parts along dimension 0, may hold values from 0 to 255
- strand_current: float32 [512], P('grp'), parts along dimension 0, may hold values from 0.5 to 2
- yoke_pos: float32 [3, 4096], P(None, ('grp', 'seg', 'yoke')), parts along dimension 1, may hold values from -1 to 1
- quad_weight: float32 [4096], P(('grp', 'seg', 'yoke')), parts along dimension 0, may hold values from 0.5 to 1.5
- panel_of: int32 [4096], P(('grp', 'seg', 'yoke')), parts along dimension 0, may hold values from 0 to 63
- panel_chi: float32 [128], P('grp'), parts along dimension 0, may hold values from 0.02 to 0.2
Outputs:
- lorentz: float32 [3, 4096], P(None, ('grp', 'seg', 'yoke')), parts along dimension 1
- moment: float32 [3, 4096], P(None, ('grp', 'seg', 'yoke')), parts along dimension 1
The draws below stay inside these ranges and needn't reach their ends.
There are 2 independent parts, one for each index of `grp`. The reference program is written for one: setup_inputs(seed, part) draws one part's arguments, and reference() takes and returns one part's arrays. A program takes and returns all parts, laid end to end along the dimension named above; each array names one. Nothing has to cross between parts.
All inputs are finite; a program needn't handle non-finite values.
Results may differ from the reference program's by a relative error of at most 0.0002.
Values sent between devices are 32-bit elements; how exact they have to be, the bound alone decides.
No kernel may reach another device: no remote copies, remote signals or barrier semaphores. Data moves between devices by JAX's collectives and lax.ppermute only.
A program may use at most 64 MiB of HBM per device.

```python
import math
import jax
import jax.numpy as jnp
from jax import lax

ITERS = 2
STRANDS = 256
PANELS = 64
SEGMENTS = 2048
YOKE_POINTS = 2048


def set_ends(drawn, own_key, smallest, largest):
    dims = drawn.shape
    index_at = [jax.random.randint(jax.random.fold_in(own_key, axis), (), 0, dims[axis]) for axis in range(len(dims))]
    drawn = drawn.at[tuple(index_at)].set(smallest)
    longest = dims.index(max(dims))
    index_at[longest] = (index_at[longest] + 1) % dims[longest]
    return drawn.at[tuple(index_at)].set(largest)


def level_of(rng, shape, cuts, least, high):
    def one(axis_at, shards_of):
        steps = jax.random.uniform(jax.random.fold_in(jax.random.fold_in(rng, 6), axis_at), (shards_of,), jnp.float32, least / len(cuts), high / len(cuts))
        return jnp.repeat(jnp.exp(steps), shape[axis_at] // shards_of).reshape((-1,) + (1,) * (len(shape) - axis_at - 1))

    level = one(*cuts[0])
    for cut in cuts[1:]:
        level = level * one(*cut)
    return level


def bell_draw(own_key, extent, deviation, most, cuts=(), kind=jnp.bfloat16):
    values = jax.random.normal(own_key, extent, jnp.float32) * deviation
    if len(cuts) > 0:
        values = level_of(own_key, extent, cuts, -0.22, 0.18) * values
    return jnp.clip(values, min=-most, max=most).astype(kind)


def setup_inputs(seed: int = 0, part: int = 0) -> dict:
    key_list = jax.random.split(jax.random.key(seed), 9)
    part_keys = jax.random.split(jax.random.fold_in(key_list[8], part), 9)
    seg_mid = jnp.clip(jax.random.uniform(part_keys[0], (3, SEGMENTS), jnp.float32, -1.0, 1.0) * level_of(part_keys[0], (3, SEGMENTS), ((1, 8),), -0.4, 0.0), -1.0, 1.0)
    seg_vec = bell_draw(part_keys[1], (3, SEGMENTS), 1.0, 6.0, ((1, 8),), jnp.float32)
    strand_of = set_ends(jax.random.randint(part_keys[2], (SEGMENTS,), 0, STRANDS), jax.random.fold_in(part_keys[2], 1), 0, STRANDS - 1).astype(jnp.int32)
    strand_current = jnp.clip(jnp.exp(jax.random.uniform(part_keys[3], (STRANDS,), jnp.float32, math.log(0.5), math.log(2.0))), 0.5, 2.0)
    yoke_pos = jnp.clip(jax.random.uniform(part_keys[4], (3, YOKE_POINTS), jnp.float32, -1.0, 1.0) * level_of(part_keys[4], (3, YOKE_POINTS), ((1, 16),), -0.4, 0.0), -1.0, 1.0)
    quad_weight = jnp.clip(jnp.exp(math.log(1.5) - 1.0986123 * jax.random.uniform(part_keys[5], (YOKE_POINTS,), jnp.float32) ** level_of(part_keys[5], (YOKE_POINTS,), ((0, 16),), -0.2, 0.2)), 0.5, 1.5)
    panel_of = set_ends(jax.random.randint(part_keys[6], (YOKE_POINTS,), 0, PANELS), jax.random.fold_in(part_keys[6], 1), 0, PANELS - 1).astype(jnp.int32)
    panel_chi = jnp.clip(jnp.exp(jax.random.uniform(part_keys[7], (PANELS,), jnp.float32, math.log(0.02), math.log(0.2))), 0.02, 0.2)
    return dict(seg_mid=seg_mid, seg_vec=seg_vec, strand_of=strand_of, strand_current=strand_current, yoke_pos=yoke_pos, quad_weight=quad_weight, panel_of=panel_of, panel_chi=panel_chi)


coil_core = 0.05
yoke_core = 0.2

def coil_kernel(targets, sources):
    delta_x = targets[0][:, None] - sources[0][None, :]
    delta_y = targets[1][:, None] - sources[1][None, :]
    delta_z = targets[2][:, None] - sources[2][None, :]
    radial = delta_x * delta_x + delta_y * delta_y + delta_z * delta_z + coil_core * coil_core
    inverse = lax.rsqrt(radial)
    weight_cube = inverse * inverse * inverse
    field_x = lax.optimization_barrier(jnp.sum(weight_cube * (sources[4][None, :] * delta_z - sources[5][None, :] * delta_y), axis=1))
    field_y = lax.optimization_barrier(jnp.sum(weight_cube * (sources[5][None, :] * delta_x - sources[3][None, :] * delta_z), axis=1))
    field_z = lax.optimization_barrier(jnp.sum(weight_cube * (sources[3][None, :] * delta_y - sources[4][None, :] * delta_x), axis=1))
    return jnp.stack([field_x, field_y, field_z], 0)

def dipole_kernel(targets, sources):
    delta_x = targets[0][:, None] - sources[0][None, :]
    delta_y = targets[1][:, None] - sources[1][None, :]
    delta_z = targets[2][:, None] - sources[2][None, :]
    radial = delta_x * delta_x + delta_y * delta_y + delta_z * delta_z
    inverse = lax.rsqrt(radial + yoke_core * yoke_core)
    fifth = inverse * inverse * inverse * inverse * inverse
    along = delta_x * sources[3][None, :] + delta_y * sources[4][None, :] + delta_z * sources[5][None, :]
    field_x = lax.optimization_barrier(jnp.sum(fifth * (3.0 * delta_x * along - radial * sources[3][None, :]), axis=1))
    field_y = lax.optimization_barrier(jnp.sum(fifth * (3.0 * delta_y * along - radial * sources[4][None, :]), axis=1))
    field_z = lax.optimization_barrier(jnp.sum(fifth * (3.0 * delta_z * along - radial * sources[5][None, :]), axis=1))
    return jnp.stack([field_x, field_y, field_z], 0)

def blocked(kernel, targets, sources, element_limit):
    columns = targets.shape[1]
    pieces = 1
    while pieces < columns and (columns % pieces != 0 or columns // pieces * sources.shape[1] > element_limit):
        pieces += 1
    if pieces == 1:
        return kernel(targets, sources)
    stacked = jnp.moveaxis(targets.reshape(3, pieces, columns // pieces), 1, 0)

    def one_block(target_block):
        return kernel(target_block, sources)
    result = lax.map(one_block, stacked)
    return jnp.moveaxis(result, 0, 1).reshape(3, columns)

def cross_rows(left_rows, right_rows):
    return jnp.stack([left_rows[1] * right_rows[2] - left_rows[2] * right_rows[1], left_rows[2] * right_rows[0] - left_rows[0] * right_rows[2], left_rows[0] * right_rows[1] - left_rows[1] * right_rows[0]], 0)

def reference(seg_mid, seg_vec, strand_of, strand_current, yoke_pos, quad_weight, panel_of, panel_chi):
    element_limit = 1 << 22
    coil_scale = 1.0 / math.sqrt(SEGMENTS)
    yoke_scale = 1.0 / math.sqrt(YOKE_POINTS)
    current = strand_current[strand_of.astype(jnp.int32)]
    carried = current[None, :] * seg_vec
    seg_pack = jnp.concatenate([seg_mid, carried], 0)
    coil_yoke = blocked(coil_kernel, yoke_pos, seg_pack, element_limit) * coil_scale
    suscept = panel_chi[panel_of.astype(jnp.int32)][None, :]
    moment = suscept * coil_yoke
    for sweep_index in range(ITERS):
        source_pack = jnp.concatenate([yoke_pos, quad_weight[None, :] * moment], 0)
        moment = suscept * (coil_yoke + blocked(dipole_kernel, yoke_pos, source_pack, element_limit) * yoke_scale)
    source_pack = jnp.concatenate([yoke_pos, quad_weight[None, :] * moment], 0)
    total_field = blocked(coil_kernel, seg_mid, seg_pack, element_limit) * coil_scale
    total_field = total_field + blocked(dipole_kernel, seg_mid, source_pack, element_limit) * yoke_scale
    lorentz = cross_rows(carried, total_field)
    return (lorentz, moment)
```

```python
import math

import jax
import jax.numpy as jnp
from jax import lax
from jax.experimental import pallas as pl
from jax.experimental.pallas import tpu as pltpu
from jax.sharding import PartitionSpec as P

ITERS = 2
VMEM_BYTES = 40 << 20


coil_core = 0.05
yoke_core = 0.2


def coil_kernel(targets, sources):
    delta_x = targets[0][:, None] - sources[0][None, :]
    delta_y = targets[1][:, None] - sources[1][None, :]
    delta_z = targets[2][:, None] - sources[2][None, :]
    radial = delta_x * delta_x + delta_y * delta_y + delta_z * delta_z + coil_core * coil_core
    inverse = lax.rsqrt(radial)
    weight_cube = inverse * inverse * inverse
    field_x = jnp.sum(
        weight_cube * (sources[4][None, :] * delta_z - sources[5][None, :] * delta_y), axis=1
    )
    field_y = jnp.sum(
        weight_cube * (sources[5][None, :] * delta_x - sources[3][None, :] * delta_z), axis=1
    )
    field_z = jnp.sum(
        weight_cube * (sources[3][None, :] * delta_y - sources[4][None, :] * delta_x), axis=1
    )
    return jnp.stack([field_x, field_y, field_z], 0)


def dipole_kernel(targets, sources):
    delta_x = targets[0][:, None] - sources[0][None, :]
    delta_y = targets[1][:, None] - sources[1][None, :]
    delta_z = targets[2][:, None] - sources[2][None, :]
    radial = delta_x * delta_x + delta_y * delta_y + delta_z * delta_z
    inverse = lax.rsqrt(radial + yoke_core * yoke_core)
    fifth = inverse * inverse * inverse * inverse * inverse
    along = (
        delta_x * sources[3][None, :]
        + delta_y * sources[4][None, :]
        + delta_z * sources[5][None, :]
    )
    field_x = jnp.sum(fifth * (3.0 * delta_x * along - radial * sources[3][None, :]), axis=1)
    field_y = jnp.sum(fifth * (3.0 * delta_y * along - radial * sources[4][None, :]), axis=1)
    field_z = jnp.sum(fifth * (3.0 * delta_z * along - radial * sources[5][None, :]), axis=1)
    return jnp.stack([field_x, field_y, field_z], 0)


def blocked(kernel, targets, sources, element_limit):
    columns = targets.shape[1]
    pieces = 1
    while pieces < columns and (
        columns % pieces != 0 or columns // pieces * sources.shape[1] > element_limit
    ):
        pieces += 1
    if pieces == 1:
        return kernel(targets, sources)
    stacked = jnp.moveaxis(targets.reshape(3, pieces, columns // pieces), 1, 0)

    def one_block(target_block):
        return kernel(target_block, sources)

    result = lax.map(one_block, stacked)
    return jnp.moveaxis(result, 0, 1).reshape(3, columns)


def fold_blocks(kernel, targets, sources, shard_len):
    columns = sources.shape[1]
    shards = columns // shard_len
    group_size = max(1, (1 << 20) // (targets.shape[1] * shard_len))
    group_size = min(group_size, shards)
    while shards % group_size != 0:
        group_size -= 1
    block_width = group_size * shard_len
    block_count = columns // block_width
    if block_count == 1:
        return kernel(targets, sources)
    stacked = jnp.moveaxis(sources.reshape(sources.shape[0], block_count, block_width), 1, 0)

    def advance(running, source_block):
        return (running + kernel(targets, source_block), None)

    result, unused = lax.scan(advance, jnp.zeros((3, targets.shape[1]), jnp.float32), stacked)
    return result


def make_fold(kernel, targets, shard_len, sources):
    return fold_blocks(kernel, targets, sources, shard_len)


def cross_rows(left_rows, right_rows):
    return jnp.stack(
        [
            left_rows[1] * right_rows[2] - left_rows[2] * right_rows[1],
            left_rows[2] * right_rows[0] - left_rows[0] * right_rows[2],
            left_rows[0] * right_rows[1] - left_rows[1] * right_rows[0],
        ],
        0,
    )


def table_lookup(indices, table):
    rows_iota = lax.broadcasted_iota(jnp.int32, (table.shape[0], indices.shape[0]), 0)
    return jnp.sum(jnp.where(indices[None, :] == rows_iota, table[:, None], 0.0), axis=0)


def far_body(seg_mid, seg_vec, strand_of, strand_current, yoke_pos, quad_weight, panel_of, panel_chi):
    seg_len = seg_mid.shape[1]
    half_len = seg_len // 2
    yoke_len = yoke_pos.shape[1]
    segments_total = seg_len * lax.axis_size("seg")
    points_total = yoke_len * lax.axis_size("seg") * lax.axis_size("yoke")
    coil_scale = 1.0 / math.sqrt(segments_total)
    yoke_scale = 1.0 / math.sqrt(points_total)
    current = table_lookup(strand_of, strand_current)
    carried = current[None, :] * seg_vec
    seg_pack = jnp.concatenate([seg_mid, carried], 0)
    suscept = table_lookup(panel_of, panel_chi)[None, :]
    half_start = lax.axis_index("yoke") * half_len
    own_mid = lax.dynamic_slice_in_dim(seg_mid, half_start, half_len, 1)
    own_carried = lax.dynamic_slice_in_dim(carried, half_start, half_len, 1)
    half_points = lax.all_gather(yoke_pos, "seg", axis=1, tiled=True)
    partial_value = blocked(coil_kernel, half_points, seg_pack, 1 << 19)
    coil_yoke = lax.psum_scatter(partial_value, "seg", scatter_dimension=1, tiled=True) * coil_scale
    coil_seg = (
        make_fold(
            coil_kernel, own_mid, seg_len, lax.all_gather(seg_pack, "seg", axis=1, tiled=True)
        )
        * coil_scale
    )

    def moment_field(targets, moment):
        source_pack = jnp.concatenate([yoke_pos, quad_weight[None, :] * moment], 0)
        gathered_sum = make_fold(
            dipole_kernel,
            targets,
            yoke_len,
            lax.all_gather(source_pack, ("seg", "yoke"), axis=1, tiled=True),
        )
        return gathered_sum * yoke_scale

    moment = suscept * coil_yoke
    for sweep_index in range(ITERS):
        moment = suscept * (coil_yoke + moment_field(yoke_pos, moment))
    total_field = coil_seg + moment_field(own_mid, moment)
    lorentz = cross_rows(own_carried, total_field)
    return (lorentz, moment)


def bf16_parts(value):
    parts = []
    for place in range(3):
        part = value.astype(jnp.bfloat16)
        parts.append(part)
        if place < 2:
            value = value - part.astype(jnp.float32)
    return parts


def split_rows(rows, split_ref):
    count = rows.shape[0]
    for place, part in enumerate(bf16_parts(rows)):
        split_ref[place * count : (place + 1) * count, :] = part


def joined(product):
    count = product.shape[0] // 3
    return product[:count] + product[count : 2 * count] + product[2 * count :]


def pick(table_ref, index_ref):
    entries = lax.broadcasted_iota(jnp.int32, (table_ref.shape[1], index_ref.shape[1]), 0)
    chosen = jnp.where(entries == index_ref[...], 1.0, 0.0)
    table = jnp.broadcast_to(table_ref[...], (8, table_ref.shape[1]))
    found = jnp.dot(
        table, chosen, precision=lax.Precision.HIGHEST, preferred_element_type=jnp.float32
    )
    return found[:1]


def pack_kernel(
    mid_ref, vec_ref, strand_ref, current_ref, pos_ref, weight_ref, panel_ref, chi_ref, out_ref
):
    half = pos_ref.shape[1]
    first = lax.axis_index("yoke") == 0
    mid = jnp.where(first, mid_ref[:, :half], mid_ref[:, half:])
    carried = pick(current_ref, strand_ref) * vec_ref[...]
    carried = jnp.where(first, carried[:, :half], carried[:, half:])
    zeros = jnp.zeros((3, half), jnp.float32)
    packed = jnp.concatenate(
        [
            pos_ref[...],
            weight_ref[...],
            pick(chi_ref, panel_ref),
            zeros,
            mid,
            carried,
            zeros[:2],
        ],
        0,
    )
    out_ref[...] = jnp.broadcast_to(packed[None], out_ref.shape)


def coil_stage(gathered_ref, row_ref, col_ref, state_ref, split_ref, *weight_refs):
    blocks, _, width = gathered_ref.shape
    total = blocks * width
    half = total // 2
    coil_scale = 1.0 / math.sqrt(total)
    positions = gathered_ref[0, 0:3, :]
    for block in range(1, blocks):
        positions = positions + gathered_ref[block, 0:3, :]
    center = jnp.sum(positions, axis=1, keepdims=True) * (1.0 / total)
    none = jnp.zeros((5, 1), jnp.float32)
    shift = jnp.concatenate([center, none, center, none], 0)
    for block in range(blocks):
        place = (block % 2) * half + (block // 2) * width
        rows = gathered_ref[block] - shift
        row_ref[:, place : place + width] = rows
        col_ref[place : place + width, :] = rows.T
    mx, my, mz, cx, cy, cz = [row_ref[8 + k : 9 + k, :] for k in range(6)]
    split_rows(
        jnp.concatenate(
            [
                cx,
                cy,
                cz,
                cy * mz - cz * my,
                cz * mx - cx * mz,
                cx * my - cy * mx,
                jnp.zeros((10, total), jnp.float32),
            ],
            0,
        ),
        split_ref,
    )
    mine = pl.ds(pl.multiple_of(lax.axis_index("yoke") * half, half), half)
    tx, ty, tz = [row_ref[k : k + 1, mine] for k in range(3)]
    depth = 256
    count = total // depth
    product = jnp.zeros((split_ref.shape[0], half), jnp.float32)

    def build(chunk):
        target = weight_refs[3 * (chunk % 2) : 3 * (chunk % 2) + 3]
        for start in range(0, depth, 32):
            at = chunk * depth + start
            dx = tx - col_ref[at : at + 32, 8:9]
            dy = ty - col_ref[at : at + 32, 9:10]
            dz = tz - col_ref[at : at + 32, 10:11]
            inverse = lax.rsqrt(dx * dx + dy * dy + dz * dz + coil_core * coil_core)
            for ref, part in zip(target, bf16_parts(inverse * inverse * inverse)):
                ref[start : start + 32, :] = part

    build(0)
    for chunk in range(count):
        if chunk + 1 < count:
            build(chunk + 1)
        rows = split_ref[:, chunk * depth : (chunk + 1) * depth]
        for ref in weight_refs[3 * (chunk % 2) : 3 * (chunk % 2) + 3]:
            product = product + jnp.dot(rows, ref[...], preferred_element_type=jnp.float32)
    sums = joined(product)
    sx, sy, sz = [sums[k : k + 1] for k in range(3)]
    field = (
        jnp.concatenate([sy * tz - sz * ty, sz * tx - sx * tz, sx * ty - sy * tx], 0) - sums[3:6]
    ) * coil_scale
    suscept = row_ref[4:5, mine]
    state_ref[...] = jnp.concatenate(
        [field, suscept * field, jnp.zeros((2, half), jnp.float32)], 0
    )


def spread_stage(row_ref, col_ref, *part_refs):
    total = row_ref.shape[1]
    half = total // 2
    mine = pl.ds(pl.multiple_of(lax.axis_index("yoke") * half, half), half)
    tx, ty, tz = [row_ref[k : k + 1, mine] for k in range(3)]
    depth = 256

    def build(chunk, carry):
        for start in range(0, depth, 32):
            at = pl.ds(pl.multiple_of(chunk * depth + start, 32), 32)
            sources = col_ref[at, :]
            dx = tx - sources[:, 0:1]
            dy = ty - sources[:, 1:2]
            dz = tz - sources[:, 2:3]
            inverse = lax.rsqrt(dx * dx + dy * dy + dz * dz + yoke_core * yoke_core)
            square = inverse * inverse
            for ref, part in zip(part_refs, bf16_parts(square * square * inverse)):
                ref[at, :] = part
        return carry

    lax.fori_loop(0, total // depth, build, 0)


def both_halves(own, other):
    first = lax.axis_index("yoke") == 0
    return jnp.concatenate([jnp.where(first, own, other), jnp.where(first, other, own)], 1)


def sweep_stage(row_ref, own_ref, other_ref, *refs):
    part_refs, (state_ref, split_ref) = refs[:3], refs[3:]
    total = row_ref.shape[1]
    half = total // 2
    yoke_scale = 1.0 / math.sqrt(total)
    moment = both_halves(own_ref[3:6, :], other_ref[3:6, :])
    strength = row_ref[3:4, :] * moment
    ux, uy, uz = [strength[k : k + 1] for k in range(3)]
    qx, qy, qz = [row_ref[k : k + 1, :] for k in range(3)]
    along = 3.0 * (qx * ux + qy * uy + qz * uz)
    square = qx * qx + qy * qy + qz * qz
    split_rows(
        jnp.concatenate(
            [
                strength,
                qx * strength,
                qy * strength,
                qz * strength,
                qx * along - square * ux,
                qy * along - square * uy,
                qz * along - square * uz,
                jnp.zeros((1, total), jnp.float32),
            ],
            0,
        ),
        split_ref,
    )
    depth = 256
    product = jnp.zeros((split_ref.shape[0], half), jnp.float32)
    for chunk in range(total // depth):
        at = slice(chunk * depth, (chunk + 1) * depth)
        rows = split_ref[:, at]
        for ref in part_refs:
            product = product + jnp.dot(rows, ref[at, :], preferred_element_type=jnp.float32)
    sums = joined(product)
    mine = pl.ds(pl.multiple_of(lax.axis_index("yoke") * half, half), half)
    target = [row_ref[k : k + 1, mine] for k in range(3)]
    tx, ty, tz = target
    plain = [sums[k : k + 1] for k in range(3)]
    tensor = [[sums[3 + 3 * a + b : 4 + 3 * a + b] for b in range(3)] for a in range(3)]
    toward = tx * plain[0] + ty * plain[1] + tz * plain[2]
    trace = tensor[0][0] + tensor[1][1] + tensor[2][2]
    lead = 3.0 * (toward - trace)
    reach = tx * tx + ty * ty + tz * tz
    fields = []
    for a in range(3):
        field = target[a] * lead - reach * plain[a] + sums[12 + a : 13 + a]
        for b in range(3):
            field = field + target[b] * (2.0 * tensor[b][a] - 3.0 * tensor[a][b])
        fields.append(field)
    coil = own_ref[0:3, :]
    fresh = row_ref[4:5, mine] * (coil + jnp.concatenate(fields, 0) * yoke_scale)
    state_ref[...] = jnp.concatenate([coil, fresh, jnp.zeros((2, half), jnp.float32)], 0)


def own_place(total, width):
    half = total // 2
    start = lax.axis_index("yoke") * half + lax.axis_index("seg") * width
    return pl.ds(pl.multiple_of(start, width), width)


def columns_of(rows):
    return jnp.concatenate([rows, jnp.zeros((5, rows.shape[1]), jnp.float32)], 0).T


def gather_lanes(terms, width):
    count = terms.shape[1] // width
    total = terms[:, :width]
    for k in range(1, count):
        total = total + terms[:, k * width : (k + 1) * width]
    return jnp.sum(total, axis=1, keepdims=True)


def rows_of(columns, width):
    table = jnp.concatenate(columns + [jnp.zeros((width, 5), jnp.float32)], 1)
    return table.T[0:3]


def segment_stage(row_ref, out_ref):
    total = row_ref.shape[1]
    width = out_ref.shape[1]
    targets = columns_of(row_ref[8:11, own_place(total, width)])
    mx, my, mz, cx, cy, cz = [row_ref[8 + k : 9 + k, :] for k in range(6)]
    found = [[], [], []]
    for start in range(0, width, 8):
        at = targets[start : start + 8]
        dx, dy, dz = at[:, 0:1] - mx, at[:, 1:2] - my, at[:, 2:3] - mz
        inverse = lax.rsqrt(dx * dx + dy * dy + dz * dz + coil_core * coil_core)
        cube = inverse * inverse * inverse
        found[0].append(gather_lanes(cube * (cy * dz - cz * dy), 128))
        found[1].append(gather_lanes(cube * (cz * dx - cx * dz), 128))
        found[2].append(gather_lanes(cube * (cx * dy - cy * dx), 128))
    field = rows_of([jnp.concatenate(each, 0) for each in found], width)
    out_ref[...] = field * (1.0 / math.sqrt(total))


def force_stage(row_ref, own_ref, other_ref, coil_ref, lorentz_ref, moment_ref):
    total = row_ref.shape[1]
    width = coil_ref.shape[1]
    segment = pl.ds(pl.multiple_of(lax.axis_index("seg") * width, width), width)
    moment_ref[...] = own_ref[3:6, segment]
    place = own_place(total, width)
    targets = columns_of(row_ref[8:11, place])
    strength = row_ref[3:4, :] * both_halves(own_ref[3:6, :], other_ref[3:6, :])
    ux, uy, uz = [strength[k : k + 1] for k in range(3)]
    qx, qy, qz = [row_ref[k : k + 1, :] for k in range(3)]
    found = [[], [], []]
    for start in range(0, width, 8):
        at = targets[start : start + 8]
        dx, dy, dz = at[:, 0:1] - qx, at[:, 1:2] - qy, at[:, 2:3] - qz
        radial = dx * dx + dy * dy + dz * dz
        inverse = lax.rsqrt(radial + yoke_core * yoke_core)
        square = inverse * inverse
        fifth = square * square * inverse
        along = 3.0 * fifth * (dx * ux + dy * uy + dz * uz)
        pull = fifth * radial
        found[0].append(gather_lanes(dx * along - pull * ux, 128))
        found[1].append(gather_lanes(dy * along - pull * uy, 128))
        found[2].append(gather_lanes(dz * along - pull * uz, 128))
    field = rows_of([jnp.concatenate(each, 0) for each in found], width)
    field = coil_ref[...] + field * (1.0 / math.sqrt(total))
    fx, fy, fz = [field[k : k + 1] for k in range(3)]
    cx, cy, cz = [row_ref[11 + k : 12 + k, place] for k in range(3)]
    lorentz_ref[...] = jnp.concatenate(
        [cy * fz - cz * fy, cz * fx - cx * fz, cx * fy - cy * fx], 0
    )


def call(kernel, outputs, scratch, *operands):
    return pl.pallas_call(
        kernel,
        out_shape=outputs,
        scratch_shapes=scratch,
        compiler_params=pltpu.CompilerParams(vmem_limit_bytes=VMEM_BYTES),
    )(*operands)


def close_body(
    seg_mid, seg_vec, strand_of, strand_current, yoke_pos, quad_weight, panel_of, panel_chi
):
    width = yoke_pos.shape[1]
    blocks = lax.axis_size("seg") * lax.axis_size("yoke")
    total = blocks * width
    half = total // 2
    shape = jax.ShapeDtypeStruct
    f32, bf16 = jnp.float32, jnp.bfloat16

    def swap(state):
        return lax.ppermute(state, "yoke", [(0, 1), (1, 0)])

    packed = call(
        pack_kernel,
        shape((blocks, 16, width), f32),
        [],
        seg_mid,
        seg_vec,
        strand_of[None],
        strand_current[None],
        yoke_pos,
        quad_weight[None],
        panel_of[None],
        panel_chi[None],
    )
    gathered = lax.all_to_all(packed, ("seg", "yoke"), 0, 0, tiled=True)
    state_shape = shape((8, half), f32)
    split_scratch = pltpu.VMEM((48, total), bf16)
    rows, columns, state = call(
        coil_stage,
        (shape((16, total), f32), shape((total, 16), f32), state_shape),
        [split_scratch] + [pltpu.VMEM((256, half), bf16)] * 6,
        gathered,
    )
    other = swap(state)
    spread = call(spread_stage, [shape((total, half), bf16)] * 3, [], rows, columns)
    for sweep in range(ITERS):
        state = call(sweep_stage, state_shape, [split_scratch], rows, state, other, *spread)
        other = swap(state)
    coil_segments = call(segment_stage, shape((3, width), f32), [], rows)
    return tuple(
        call(
            force_stage,
            (shape((3, width), f32), shape((3, width), f32)),
            [],
            rows,
            state,
            other,
            coil_segments,
        )
    )


def body(*arrays):
    seg_len, yoke_len = arrays[0].shape[1], arrays[4].shape[1]
    blocks = lax.axis_size("seg") * lax.axis_size("yoke")
    close = seg_len == 256 and yoke_len == 128 and lax.axis_size("yoke") == 2 and blocks == 16
    return (close_body if close else far_body)(*arrays)


def solution(mesh):
    placed = (
        P(None, ("grp", "seg")),
        P(None, ("grp", "seg")),
        P(("grp", "seg")),
        P("grp"),
        P(None, ("grp", "seg", "yoke")),
        P(("grp", "seg", "yoke")),
        P(("grp", "seg", "yoke")),
        P("grp"),
    )
    return jax.shard_map(
        body,
        mesh=mesh,
        in_specs=placed,
        out_specs=(P(None, ("grp", "seg", "yoke")), P(None, ("grp", "seg", "yoke"))),
        check_vma=False,
    )
```

```python
import math

import jax
import jax.numpy as jnp
from jax import lax
from jax.experimental import pallas as pl
from jax.experimental.pallas import tpu as pltpu
from jax.sharding import PartitionSpec as P

ITERS = 2
VMEM_BYTES = 16 << 20


coil_core = 0.05
yoke_core = 0.2


def coil_kernel(targets, sources):
    delta_x = targets[0][:, None] - sources[0][None, :]
    delta_y = targets[1][:, None] - sources[1][None, :]
    delta_z = targets[2][:, None] - sources[2][None, :]
    radial = delta_x * delta_x + delta_y * delta_y + delta_z * delta_z + coil_core * coil_core
    inverse = lax.rsqrt(radial)
    weight_cube = inverse * inverse * inverse
    field_x = jnp.sum(
        weight_cube * (sources[4][None, :] * delta_z - sources[5][None, :] * delta_y), axis=1
    )
    field_y = jnp.sum(
        weight_cube * (sources[5][None, :] * delta_x - sources[3][None, :] * delta_z), axis=1
    )
    field_z = jnp.sum(
        weight_cube * (sources[3][None, :] * delta_y - sources[4][None, :] * delta_x), axis=1
    )
    return jnp.stack([field_x, field_y, field_z], 0)


def dipole_kernel(targets, sources):
    delta_x = targets[0][:, None] - sources[0][None, :]
    delta_y = targets[1][:, None] - sources[1][None, :]
    delta_z = targets[2][:, None] - sources[2][None, :]
    radial = delta_x * delta_x + delta_y * delta_y + delta_z * delta_z
    inverse = lax.rsqrt(radial + yoke_core * yoke_core)
    fifth = inverse * inverse * inverse * inverse * inverse
    along = (
        delta_x * sources[3][None, :]
        + delta_y * sources[4][None, :]
        + delta_z * sources[5][None, :]
    )
    field_x = jnp.sum(fifth * (3.0 * delta_x * along - radial * sources[3][None, :]), axis=1)
    field_y = jnp.sum(fifth * (3.0 * delta_y * along - radial * sources[4][None, :]), axis=1)
    field_z = jnp.sum(fifth * (3.0 * delta_z * along - radial * sources[5][None, :]), axis=1)
    return jnp.stack([field_x, field_y, field_z], 0)


def blocked(kernel, targets, sources, element_limit):
    columns = targets.shape[1]
    pieces = 1
    while pieces < columns and (
        columns % pieces != 0 or columns // pieces * sources.shape[1] > element_limit
    ):
        pieces += 1
    if pieces == 1:
        return kernel(targets, sources)
    stacked = jnp.moveaxis(targets.reshape(3, pieces, columns // pieces), 1, 0)

    def one_block(target_block):
        return kernel(target_block, sources)

    result = lax.map(one_block, stacked)
    return jnp.moveaxis(result, 0, 1).reshape(3, columns)


def fold_blocks(kernel, targets, sources, shard_len):
    columns = sources.shape[1]
    shards = columns // shard_len
    group_size = max(1, (1 << 20) // (targets.shape[1] * shard_len))
    group_size = min(group_size, shards)
    while shards % group_size != 0:
        group_size -= 1
    block_width = group_size * shard_len
    block_count = columns // block_width
    if block_count == 1:
        return kernel(targets, sources)
    stacked = jnp.moveaxis(sources.reshape(sources.shape[0], block_count, block_width), 1, 0)

    def advance(running, source_block):
        return (running + kernel(targets, source_block), None)

    result, unused = lax.scan(advance, jnp.zeros((3, targets.shape[1]), jnp.float32), stacked)
    return result


def make_fold(kernel, targets, shard_len, sources):
    return fold_blocks(kernel, targets, sources, shard_len)


def cross_rows(left_rows, right_rows):
    return jnp.stack(
        [
            left_rows[1] * right_rows[2] - left_rows[2] * right_rows[1],
            left_rows[2] * right_rows[0] - left_rows[0] * right_rows[2],
            left_rows[0] * right_rows[1] - left_rows[1] * right_rows[0],
        ],
        0,
    )


def table_lookup(indices, table):
    rows_iota = lax.broadcasted_iota(jnp.int32, (table.shape[0], indices.shape[0]), 0)
    return jnp.sum(jnp.where(indices[None, :] == rows_iota, table[:, None], 0.0), axis=0)


def far_body(seg_mid, seg_vec, strand_of, strand_current, yoke_pos, quad_weight, panel_of, panel_chi):
    seg_len = seg_mid.shape[1]
    half_len = seg_len // 2
    yoke_len = yoke_pos.shape[1]
    segments_total = seg_len * lax.axis_size("seg")
    points_total = yoke_len * lax.axis_size("seg") * lax.axis_size("yoke")
    coil_scale = 1.0 / math.sqrt(segments_total)
    yoke_scale = 1.0 / math.sqrt(points_total)
    current = table_lookup(strand_of, strand_current)
    carried = current[None, :] * seg_vec
    seg_pack = jnp.concatenate([seg_mid, carried], 0)
    suscept = table_lookup(panel_of, panel_chi)[None, :]
    half_start = lax.axis_index("yoke") * half_len
    own_mid = lax.dynamic_slice_in_dim(seg_mid, half_start, half_len, 1)
    own_carried = lax.dynamic_slice_in_dim(carried, half_start, half_len, 1)
    half_points = lax.all_gather(yoke_pos, "seg", axis=1, tiled=True)
    partial_value = blocked(coil_kernel, half_points, seg_pack, 1 << 19)
    coil_yoke = lax.psum_scatter(partial_value, "seg", scatter_dimension=1, tiled=True) * coil_scale
    coil_seg = (
        make_fold(
            coil_kernel, own_mid, seg_len, lax.all_gather(seg_pack, "seg", axis=1, tiled=True)
        )
        * coil_scale
    )

    def moment_field(targets, moment):
        source_pack = jnp.concatenate([yoke_pos, quad_weight[None, :] * moment], 0)
        gathered_sum = make_fold(
            dipole_kernel,
            targets,
            yoke_len,
            lax.all_gather(source_pack, ("seg", "yoke"), axis=1, tiled=True),
        )
        return gathered_sum * yoke_scale

    moment = suscept * coil_yoke
    for sweep_index in range(ITERS):
        moment = suscept * (coil_yoke + moment_field(yoke_pos, moment))
    total_field = coil_seg + moment_field(own_mid, moment)
    lorentz = cross_rows(own_carried, total_field)
    return (lorentz, moment)


def bf16_parts(value):
    parts = []
    for place in range(3):
        part = value.astype(jnp.bfloat16)
        parts.append(part)
        if place < 2:
            value = value - part.astype(jnp.float32)
    return parts


def split_rows(rows, split_ref):
    count = rows.shape[0]
    for place, part in enumerate(bf16_parts(rows)):
        split_ref[place * count : (place + 1) * count, :] = part


def joined(product):
    count = product.shape[0] // 3
    return product[:count] + product[count : 2 * count] + product[2 * count :]


def pick(table_ref, index_ref):
    entries = lax.broadcasted_iota(jnp.int32, (table_ref.shape[1], index_ref.shape[1]), 0)
    chosen = jnp.where(entries == index_ref[...], 1.0, 0.0)
    table = jnp.broadcast_to(table_ref[...], (8, table_ref.shape[1]))
    found = jnp.dot(
        table, chosen, precision=lax.Precision.HIGHEST, preferred_element_type=jnp.float32
    )
    return found[:1]


def pack_kernel(*refs):
    sources, (out_ref, chi_ref), held, sems = refs[:8], refs[8:10], refs[10:18], refs[18]
    copies = [
        pltpu.make_async_copy(source, target, sems.at[place])
        for place, (source, target) in enumerate(zip(sources, held))
    ]
    for copy in copies:
        copy.start()
    for copy in copies:
        copy.wait()
    mid_ref, vec_ref, strand_ref, current_ref, pos_ref, weight_ref, panel_ref, table_ref = held
    half = pos_ref.shape[1]
    first = lax.axis_index("yoke") == 0
    mid = jnp.where(first, mid_ref[:, :half], mid_ref[:, half:])
    carried = pick(current_ref, strand_ref) * vec_ref[...]
    carried = jnp.where(first, carried[:, :half], carried[:, half:])
    suscept = pick(table_ref, panel_ref)
    chi_ref[...] = suscept
    rows = [pos_ref[k : k + 1, :] for k in range(3)]
    rows += [mid[k : k + 1] for k in range(3)]
    rows += [weight_ref[...] * suscept]
    rows += [carried[k : k + 1] for k in range(3)]
    for block in range(out_ref.shape[0]):
        for place, row in enumerate(rows):
            out_ref[block, :, place * half : (place + 1) * half] = row


def half_at(half):
    return pl.ds(pl.multiple_of(lax.axis_index("yoke") * half, half), half)


def own_at(half, width):
    start = lax.axis_index("yoke") * half + lax.axis_index("seg") * width
    return pl.ds(pl.multiple_of(start, width), width)


def target_rows(row_ref, half, width):
    near, own = half_at(half), own_at(half, width)
    return [
        jnp.concatenate([row_ref[k : k + 1, near], row_ref[3 + k : 4 + k, own]], 1)
        for k in range(3)
    ]


def fill(targets, col_ref, at, first, core, power, part_refs, start):
    sources = col_ref[at, :]
    dx, dy, dz = [targets[k] - sources[:, first + k : first + k + 1] for k in range(3)]
    inverse = lax.rsqrt(dx * dx + dy * dy + dz * dz + core * core)
    square = inverse * inverse
    value = square * inverse if power == 3 else square * square * inverse
    for ref, part in zip(part_refs, bf16_parts(value)):
        ref[start : start + value.shape[0], :] = part


def coil_stage(
    gathered_ref, row_ref, col_ref, field_ref, segment_ref, split_ref, *weight_refs
):
    blocks = gathered_ref.shape[0]
    total = row_ref.shape[1]
    half, width = total // 2, total // blocks
    for block in range(blocks):
        place = (block % 2) * half + (block // 2) * width
        for k in range(10):
            row_ref[k : k + 1, place : place + width] = gathered_ref[
                block, :, k * width : (k + 1) * width
            ]
    center = jnp.sum(row_ref[0:3, :], axis=1, keepdims=True) * (1.0 / total)
    shift = jnp.concatenate([center, center, jnp.zeros((2, 1), jnp.float32)], 0)
    row_ref[0:8, :] = row_ref[0:8, :] - shift
    for block in range(blocks):
        at = slice(block * width, (block + 1) * width)
        col_ref[at, :] = row_ref[0:8, at].T
    mx, my, mz = [row_ref[3 + k : 4 + k, :] for k in range(3)]
    cx, cy, cz = [row_ref[7 + k : 8 + k, :] for k in range(3)]
    split_rows(
        jnp.concatenate(
            [
                cx,
                cy,
                cz,
                cy * mz - cz * my,
                cz * mx - cx * mz,
                cx * my - cy * mx,
                jnp.zeros((10, total), jnp.float32),
            ],
            0,
        ),
        split_ref,
    )
    targets = target_rows(row_ref, half, width)
    tx, ty, tz = targets
    depth, step = 256, 32
    count = total // depth
    product = jnp.zeros((split_ref.shape[0], half + width), jnp.float32)

    def build(chunk):
        part_refs = weight_refs[3 * (chunk % 2) : 3 * (chunk % 2) + 3]
        for start in range(0, depth, step):
            at = slice(chunk * depth + start, chunk * depth + start + step)
            fill(targets, col_ref, at, 3, coil_core, 3, part_refs, start)

    build(0)
    for chunk in range(count):
        if chunk + 1 < count:
            build(chunk + 1)
        rows = split_ref[:, chunk * depth : (chunk + 1) * depth]
        for ref in weight_refs[3 * (chunk % 2) : 3 * (chunk % 2) + 3]:
            product = product + jnp.dot(rows, ref[...], preferred_element_type=jnp.float32)
    sums = joined(product)
    sx, sy, sz = [sums[k : k + 1] for k in range(3)]
    field = jnp.concatenate([sy * tz - sz * ty, sz * tx - sx * tz, sx * ty - sy * tx], 0)
    field = (field - sums[3:6]) * (1.0 / math.sqrt(total))
    field_ref[...] = field[:, :half]
    segment_ref[...] = field[:, half:]


def spread_stage(row_ref, col_ref, *part_refs):
    total, columns = part_refs[0].shape
    targets = target_rows(row_ref, total // 2, columns - total // 2)
    step = 32
    for start in range(0, total, step):
        at = slice(start, start + step)
        fill(targets, col_ref, at, 0, yoke_core, 5, part_refs, start)


def source_rows(row_ref, own_ref, other_ref, split_ref):
    total = row_ref.shape[1]
    first = lax.axis_index("yoke") == 0
    own, other = own_ref[...], other_ref[...]
    field = jnp.concatenate([jnp.where(first, own, other), jnp.where(first, other, own)], 1)
    strength = row_ref[6:7, :] * field
    ux, uy, uz = [strength[k : k + 1] for k in range(3)]
    qx, qy, qz = [row_ref[k : k + 1, :] for k in range(3)]
    along = 3.0 * (qx * ux + qy * uy + qz * uz)
    square = qx * qx + qy * qy + qz * qz
    split_rows(
        jnp.concatenate(
            [
                strength,
                qx * strength,
                qy * strength,
                qz * strength,
                qx * along - square * ux,
                qy * along - square * uy,
                qz * along - square * uz,
                jnp.zeros((1, total), jnp.float32),
            ],
            0,
        ),
        split_ref,
    )


def dipole_field(targets, split_ref, part_refs, columns):
    total = split_ref.shape[1]
    depth = 256
    product = jnp.zeros((split_ref.shape[0], targets[0].shape[1]), jnp.float32)
    for start in range(0, total, depth):
        rows = split_ref[:, start : start + depth]
        for ref in part_refs:
            product = product + jnp.dot(
                rows, ref[start : start + depth, columns], preferred_element_type=jnp.float32
            )
    sums = joined(product)
    tx, ty, tz = targets
    plain = [sums[k : k + 1] for k in range(3)]
    tensor = [[sums[3 + 3 * a + b : 4 + 3 * a + b] for b in range(3)] for a in range(3)]
    toward = tx * plain[0] + ty * plain[1] + tz * plain[2]
    trace = tensor[0][0] + tensor[1][1] + tensor[2][2]
    lead = 3.0 * (toward - trace)
    reach = tx * tx + ty * ty + tz * tz
    fields = []
    for a in range(3):
        field = targets[a] * lead - reach * plain[a] + sums[12 + a : 13 + a]
        for b in range(3):
            field = field + targets[b] * (2.0 * tensor[b][a] - 3.0 * tensor[a][b])
        fields.append(field)
    return jnp.concatenate(fields, 0) * (1.0 / math.sqrt(total))


def sweep_stage(row_ref, coil_ref, own_ref, other_ref, *refs):
    part_refs, (field_ref, split_ref) = refs[:3], refs[3:]
    half = coil_ref.shape[1]
    source_rows(row_ref, own_ref, other_ref, split_ref)
    near = half_at(half)
    targets = [row_ref[k : k + 1, near] for k in range(3)]
    field_ref[...] = coil_ref[...] + dipole_field(
        targets, split_ref, part_refs, slice(0, half)
    )


def force_stage(row_ref, chi_ref, segment_ref, own_ref, other_ref, *refs):
    part_refs, (lorentz_ref, moment_ref, split_ref) = refs[:3], refs[3:]
    half, width = own_ref.shape[1], chi_ref.shape[1]
    at = pl.ds(pl.multiple_of(lax.axis_index("seg") * width, width), width)
    moment_ref[...] = chi_ref[...] * own_ref[:, at]
    source_rows(row_ref, own_ref, other_ref, split_ref)
    own = own_at(half, width)
    targets = [row_ref[3 + k : 4 + k, own] for k in range(3)]
    field = segment_ref[...] + dipole_field(
        targets, split_ref, part_refs, slice(half, half + width)
    )
    fx, fy, fz = [field[k : k + 1] for k in range(3)]
    cx, cy, cz = [row_ref[7 + k : 8 + k, own] for k in range(3)]
    lorentz_ref[...] = jnp.concatenate(
        [cy * fz - cz * fy, cz * fx - cx * fz, cx * fy - cy * fx], 0
    )


def call(kernel, outputs, scratch, *operands, limit=VMEM_BYTES, **options):
    return pl.pallas_call(
        kernel,
        out_shape=outputs,
        scratch_shapes=scratch,
        compiler_params=pltpu.CompilerParams(vmem_limit_bytes=limit),
        **options,
    )(*operands)


def close_body(
    seg_mid, seg_vec, strand_of, strand_current, yoke_pos, quad_weight, panel_of, panel_chi
):
    width = yoke_pos.shape[1]
    blocks = lax.axis_size("seg") * lax.axis_size("yoke")
    total = blocks * width
    half = total // 2
    f32, bf16 = jnp.float32, jnp.bfloat16

    def shape(*dims, kind=f32):
        return jax.ShapeDtypeStruct(dims, kind)

    def swap(field):
        return lax.ppermute(field, "yoke", [(0, 1), (1, 0)])

    arrays = [
        seg_mid,
        seg_vec,
        strand_of[None],
        strand_current[None],
        yoke_pos,
        quad_weight[None],
        panel_of[None],
        panel_chi[None],
    ]
    arrays = [pltpu.with_memory_space_constraint(each, pltpu.HBM) for each in arrays]
    packed, chi = call(
        pack_kernel,
        (shape(blocks, 1, 10 * width), shape(1, width)),
        [pltpu.VMEM(each.shape, each.dtype) for each in arrays]
        + [pltpu.SemaphoreType.DMA((len(arrays),))],
        *arrays,
        in_specs=[pl.BlockSpec(memory_space=pltpu.HBM)] * len(arrays),
    )
    gathered = lax.all_to_all(packed, ("seg", "yoke"), 0, 0, tiled=True)
    split_scratch = pltpu.VMEM((48, total), bf16)
    rows, columns, coil, segments = call(
        coil_stage,
        (shape(16, total), shape(total, 8), shape(3, half), shape(3, width)),
        [split_scratch] + [pltpu.VMEM((256, half + width), bf16)] * 6,
        gathered,
    )
    own, other = coil, swap(coil)
    spread = call(spread_stage, [shape(total, half + width, kind=bf16)] * 3, [], rows, columns)
    for sweep in range(ITERS):
        own = call(
            sweep_stage, shape(3, half), [split_scratch], rows, coil, own, other, *spread
        )
        other = swap(own)
    outputs = (shape(3, width), shape(3, width))
    return tuple(
        call(
            force_stage, outputs, [split_scratch], rows, chi, segments, own, other, *spread
        )
    )


def body(*arrays):
    seg_len, yoke_len = arrays[0].shape[1], arrays[4].shape[1]
    blocks = lax.axis_size("seg") * lax.axis_size("yoke")
    close = seg_len == 256 and yoke_len == 128 and lax.axis_size("yoke") == 2 and blocks == 16
    return (close_body if close else far_body)(*arrays)


def solution(mesh):
    placed = (
        P(None, ("grp", "seg")),
        P(None, ("grp", "seg")),
        P(("grp", "seg")),
        P("grp"),
        P(None, ("grp", "seg", "yoke")),
        P(("grp", "seg", "yoke")),
        P(("grp", "seg", "yoke")),
        P("grp"),
    )
    return jax.shard_map(
        body,
        mesh=mesh,
        in_specs=placed,
        out_specs=(P(None, ("grp", "seg", "yoke")), P(None, ("grp", "seg", "yoke"))),
        check_vma=False,
    )
```

```python
import math

import jax
import jax.numpy as jnp
from jax import lax
from jax.experimental import pallas as pl
from jax.experimental.pallas import tpu as pltpu
from jax.sharding import PartitionSpec as P

ITERS = 2
VMEM_BYTES = 16 << 20


coil_core = 0.05
yoke_core = 0.2


def coil_kernel(targets, sources):
    delta_x = targets[0][:, None] - sources[0][None, :]
    delta_y = targets[1][:, None] - sources[1][None, :]
    delta_z = targets[2][:, None] - sources[2][None, :]
    radial = delta_x * delta_x + delta_y * delta_y + delta_z * delta_z + coil_core * coil_core
    inverse = lax.rsqrt(radial)
    weight_cube = inverse * inverse * inverse
    field_x = jnp.sum(
        weight_cube * (sources[4][None, :] * delta_z - sources[5][None, :] * delta_y), axis=1
    )
    field_y = jnp.sum(
        weight_cube * (sources[5][None, :] * delta_x - sources[3][None, :] * delta_z), axis=1
    )
    field_z = jnp.sum(
        weight_cube * (sources[3][None, :] * delta_y - sources[4][None, :] * delta_x), axis=1
    )
    return jnp.stack([field_x, field_y, field_z], 0)


def dipole_kernel(targets, sources):
    delta_x = targets[0][:, None] - sources[0][None, :]
    delta_y = targets[1][:, None] - sources[1][None, :]
    delta_z = targets[2][:, None] - sources[2][None, :]
    radial = delta_x * delta_x + delta_y * delta_y + delta_z * delta_z
    inverse = lax.rsqrt(radial + yoke_core * yoke_core)
    fifth = inverse * inverse * inverse * inverse * inverse
    along = (
        delta_x * sources[3][None, :]
        + delta_y * sources[4][None, :]
        + delta_z * sources[5][None, :]
    )
    field_x = jnp.sum(fifth * (3.0 * delta_x * along - radial * sources[3][None, :]), axis=1)
    field_y = jnp.sum(fifth * (3.0 * delta_y * along - radial * sources[4][None, :]), axis=1)
    field_z = jnp.sum(fifth * (3.0 * delta_z * along - radial * sources[5][None, :]), axis=1)
    return jnp.stack([field_x, field_y, field_z], 0)


def blocked(kernel, targets, sources, element_limit):
    columns = targets.shape[1]
    pieces = 1
    while pieces < columns and (
        columns % pieces != 0 or columns // pieces * sources.shape[1] > element_limit
    ):
        pieces += 1
    if pieces == 1:
        return kernel(targets, sources)
    stacked = jnp.moveaxis(targets.reshape(3, pieces, columns // pieces), 1, 0)

    def one_block(target_block):
        return kernel(target_block, sources)

    result = lax.map(one_block, stacked)
    return jnp.moveaxis(result, 0, 1).reshape(3, columns)


def fold_blocks(kernel, targets, sources, shard_len):
    columns = sources.shape[1]
    shards = columns // shard_len
    group_size = max(1, (1 << 20) // (targets.shape[1] * shard_len))
    group_size = min(group_size, shards)
    while shards % group_size != 0:
        group_size -= 1
    block_width = group_size * shard_len
    block_count = columns // block_width
    if block_count == 1:
        return kernel(targets, sources)
    stacked = jnp.moveaxis(sources.reshape(sources.shape[0], block_count, block_width), 1, 0)

    def advance(running, source_block):
        return (running + kernel(targets, source_block), None)

    result, unused = lax.scan(advance, jnp.zeros((3, targets.shape[1]), jnp.float32), stacked)
    return result


def make_fold(kernel, targets, shard_len, sources):
    return fold_blocks(kernel, targets, sources, shard_len)


def cross_rows(left_rows, right_rows):
    return jnp.stack(
        [
            left_rows[1] * right_rows[2] - left_rows[2] * right_rows[1],
            left_rows[2] * right_rows[0] - left_rows[0] * right_rows[2],
            left_rows[0] * right_rows[1] - left_rows[1] * right_rows[0],
        ],
        0,
    )


def table_lookup(indices, table):
    rows_iota = lax.broadcasted_iota(jnp.int32, (table.shape[0], indices.shape[0]), 0)
    return jnp.sum(jnp.where(indices[None, :] == rows_iota, table[:, None], 0.0), axis=0)


def far_body(seg_mid, seg_vec, strand_of, strand_current, yoke_pos, quad_weight, panel_of, panel_chi):
    seg_len = seg_mid.shape[1]
    half_len = seg_len // 2
    yoke_len = yoke_pos.shape[1]
    segments_total = seg_len * lax.axis_size("seg")
    points_total = yoke_len * lax.axis_size("seg") * lax.axis_size("yoke")
    coil_scale = 1.0 / math.sqrt(segments_total)
    yoke_scale = 1.0 / math.sqrt(points_total)
    current = table_lookup(strand_of, strand_current)
    carried = current[None, :] * seg_vec
    seg_pack = jnp.concatenate([seg_mid, carried], 0)
    suscept = table_lookup(panel_of, panel_chi)[None, :]
    half_start = lax.axis_index("yoke") * half_len
    own_mid = lax.dynamic_slice_in_dim(seg_mid, half_start, half_len, 1)
    own_carried = lax.dynamic_slice_in_dim(carried, half_start, half_len, 1)
    half_points = lax.all_gather(yoke_pos, "seg", axis=1, tiled=True)
    partial_value = blocked(coil_kernel, half_points, seg_pack, 1 << 19)
    coil_yoke = lax.psum_scatter(partial_value, "seg", scatter_dimension=1, tiled=True) * coil_scale
    coil_seg = (
        make_fold(
            coil_kernel, own_mid, seg_len, lax.all_gather(seg_pack, "seg", axis=1, tiled=True)
        )
        * coil_scale
    )

    def moment_field(targets, moment):
        source_pack = jnp.concatenate([yoke_pos, quad_weight[None, :] * moment], 0)
        gathered_sum = make_fold(
            dipole_kernel,
            targets,
            yoke_len,
            lax.all_gather(source_pack, ("seg", "yoke"), axis=1, tiled=True),
        )
        return gathered_sum * yoke_scale

    moment = suscept * coil_yoke
    for sweep_index in range(ITERS):
        moment = suscept * (coil_yoke + moment_field(yoke_pos, moment))
    total_field = coil_seg + moment_field(own_mid, moment)
    lorentz = cross_rows(own_carried, total_field)
    return (lorentz, moment)


def bf16_parts(value, count):
    parts = []
    for place in range(count):
        part = value.astype(jnp.bfloat16)
        parts.append(part)
        if place + 1 < count:
            value = value - part.astype(jnp.float32)
    return parts


def split_rows(rows, split_ref):
    count = rows.shape[0]
    for place, part in enumerate(bf16_parts(rows, 3)):
        split_ref[place * count : (place + 1) * count, :] = part


def joined(product):
    count = product.shape[0] // 3
    return product[:count] + product[count : 2 * count] + product[2 * count :]


def pick(table_ref, index_ref):
    entries = lax.broadcasted_iota(jnp.int32, (table_ref.shape[1], index_ref.shape[1]), 0)
    chosen = jnp.where(entries == index_ref[...], 1.0, 0.0)
    table = jnp.broadcast_to(table_ref[...], (8, table_ref.shape[1]))
    found = jnp.dot(
        table, chosen, precision=lax.Precision.HIGHEST, preferred_element_type=jnp.float32
    )
    return found[:1]


def pack_kernel(*refs):
    sources, (out_ref, chi_ref), held, sems = refs[:8], refs[8:10], refs[10:18], refs[18]
    copies = [
        pltpu.make_async_copy(source, target, sems.at[place])
        for place, (source, target) in enumerate(zip(sources, held))
    ]
    for copy in copies:
        copy.start()
    for copy in copies:
        copy.wait()
    mid_ref, vec_ref, strand_ref, current_ref, pos_ref, weight_ref, panel_ref, table_ref = held
    half = pos_ref.shape[1]
    first = lax.axis_index("yoke") == 0
    mid = jnp.where(first, mid_ref[:, :half], mid_ref[:, half:])
    carried = pick(current_ref, strand_ref) * vec_ref[...]
    carried = jnp.where(first, carried[:, :half], carried[:, half:])
    suscept = pick(table_ref, panel_ref)
    chi_ref[...] = suscept
    rows = [pos_ref[k : k + 1, :] for k in range(3)]
    rows += [mid[k : k + 1] for k in range(3)]
    rows += [weight_ref[...] * suscept]
    rows += [carried[k : k + 1] for k in range(3)]
    for block in range(out_ref.shape[0]):
        for place, row in enumerate(rows):
            out_ref[block, :, place * half : (place + 1) * half] = row


def times(rows, matrix_parts, transposed=False):
    contracted = ((1,), (1 if transposed else 0,))
    total = None
    for part in matrix_parts:
        product = lax.dot_general(
            rows, part, (contracted, ((), ())), preferred_element_type=jnp.float32
        )
        total = product if total is None else total + product
    return total


def power_parts(deltas, core, power):
    dx, dy, dz = deltas
    inverse = lax.rsqrt(dx * dx + dy * dy + dz * dz + core * core)
    square = inverse * inverse
    return bf16_parts(square * inverse if power == 3 else square * square * inverse, 2)


def deltas_of(rows, columns, first):
    return [rows[k] - columns[:, first + k : first + k + 1] for k in range(3)]


def coil_rows(row_ref):
    mx, my, mz = [row_ref[3 + k : 4 + k, :] for k in range(3)]
    cx, cy, cz = [row_ref[7 + k : 8 + k, :] for k in range(3)]
    blank = jnp.zeros((10, row_ref.shape[1]), jnp.float32)
    crossed = [cy * mz - cz * my, cz * mx - cx * mz, cx * my - cy * mx]
    return jnp.concatenate([cx, cy, cz] + crossed + [blank], 0)


def coil_field(product, targets, total):
    sums = joined(product)
    tx, ty, tz = targets
    sx, sy, sz = [sums[k : k + 1] for k in range(3)]
    field = jnp.concatenate([sy * tz - sz * ty, sz * tx - sx * tz, sx * ty - sy * tx], 0)
    return (field - sums[3:6]) * (1.0 / math.sqrt(total))


def coil_stage(gathered_ref, row_ref, col_ref, split_ref, field_ref, *weight_refs):
    blocks = gathered_ref.shape[0]
    total = row_ref.shape[1]
    half, width = total // 2, total // blocks
    core = lax.axis_index("yoke")
    for block in range(blocks):
        near = block < blocks // 2
        source = 2 * (block % (blocks // 2)) + (core if near else 1 - core)
        for k in range(10):
            row_ref[k : k + 1, block * width : (block + 1) * width] = gathered_ref[
                source, :, k * width : (k + 1) * width
            ]
    center = jnp.sum(row_ref[0:3, :], axis=1, keepdims=True) * (1.0 / total)
    shift = jnp.concatenate([center, center, jnp.zeros((2, 1), jnp.float32)], 0)
    row_ref[0:8, :] = row_ref[0:8, :] - shift
    for block in range(blocks):
        at = slice(block * width, (block + 1) * width)
        col_ref[at, :] = row_ref[0:8, at].T
    split_rows(coil_rows(row_ref), split_ref)
    targets = [row_ref[k : k + 1, :half] for k in range(3)]
    depth, step = 256, 32
    count = total // depth
    product = jnp.zeros((split_ref.shape[0], half), jnp.float32)

    def build(chunk):
        part_refs = weight_refs[2 * (chunk % 2) : 2 * (chunk % 2) + 2]
        for start in range(0, depth, step):
            sources = col_ref[chunk * depth + start : chunk * depth + start + step, :]
            parts = power_parts(deltas_of(targets, sources, 3), coil_core, 3)
            for ref, part in zip(part_refs, parts):
                ref[start : start + step, :] = part

    build(0)
    for chunk in range(count):
        if chunk + 1 < count:
            build(chunk + 1)
        rows = split_ref[:, chunk * depth : (chunk + 1) * depth]
        part_refs = weight_refs[2 * (chunk % 2) : 2 * (chunk % 2) + 2]
        product = product + times(rows, [ref[...] for ref in part_refs])
    field_ref[...] = coil_field(product, targets, total)


def plan(total):
    depth = total // 8
    place, rows = 0, []
    for block in range(4):
        both = list(range(block + 1, 4)) + [4 + (block + 1) % 4]
        both += [6 + block] if block < 2 else []
        targets = [block] + both + [4 + block]
        rows.append((block, place, targets))
        place += len(targets)
    return depth, place, rows


def lanes_of(array, blocks, depth):
    return jnp.concatenate([array[:, k * depth : (k + 1) * depth] for k in blocks], 1)


def spread_stage(row_ref, col_ref, *part_refs):
    depth, _, rows = plan(row_ref.shape[1])
    step = 32
    for block, place, blocks in rows:
        targets = [lanes_of(row_ref[k : k + 1, :], blocks, depth) for k in range(3)]
        lanes = slice(place * depth, (place + len(blocks)) * depth)
        for start in range(0, depth, step):
            sources = col_ref[block * depth + start : block * depth + start + step, :]
            parts = power_parts(deltas_of(targets, sources, 0), yoke_core, 5)
            for ref, part in zip(part_refs, parts):
                ref[start : start + step, lanes] = part


def source_rows(row_ref, field, split_ref):
    strength = row_ref[6:7, :] * field
    ux, uy, uz = [strength[k : k + 1] for k in range(3)]
    qx, qy, qz = [row_ref[k : k + 1, :] for k in range(3)]
    along = 3.0 * (qx * ux + qy * uy + qz * uz)
    square = qx * qx + qy * qy + qz * qz
    split_rows(
        jnp.concatenate(
            [
                strength,
                qx * strength,
                qy * strength,
                qz * strength,
                qx * along - square * ux,
                qy * along - square * uy,
                qz * along - square * uz,
                jnp.zeros((1, row_ref.shape[1]), jnp.float32),
            ],
            0,
        ),
        split_ref,
    )


def dipole_field(product, targets, total):
    sums = joined(product)
    tx, ty, tz = targets
    plain = [sums[k : k + 1] for k in range(3)]
    tensor = [[sums[3 + 3 * a + b : 4 + 3 * a + b] for b in range(3)] for a in range(3)]
    toward = tx * plain[0] + ty * plain[1] + tz * plain[2]
    trace = tensor[0][0] + tensor[1][1] + tensor[2][2]
    lead = 3.0 * (toward - trace)
    reach = tx * tx + ty * ty + tz * tz
    fields = []
    for a in range(3):
        field = targets[a] * lead - reach * plain[a] + sums[12 + a : 13 + a]
        for b in range(3):
            field = field + targets[b] * (2.0 * tensor[b][a] - 3.0 * tensor[a][b])
        fields.append(field)
    return jnp.concatenate(fields, 0) * (1.0 / math.sqrt(total))


def whole_field(own_coil_ref, other_coil_ref, partial_refs):
    field = jnp.concatenate([own_coil_ref[...], other_coil_ref[...]], 1)
    if partial_refs:
        own, other = partial_refs
        half = own.shape[1] // 2
        field = field + own[...]
        field = field + jnp.concatenate([other[:, half:], other[:, :half]], 1)
    return field


def sweep_stage(row_ref, own_coil_ref, other_coil_ref, *refs):
    partial_refs, part_refs, (out_ref, split_ref) = refs[:-4], refs[-4:-2], refs[-2:]
    total = row_ref.shape[1]
    source_rows(row_ref, whole_field(own_coil_ref, other_coil_ref, partial_refs), split_ref)
    depth, _, rows = plan(total)
    product = [None] * 8

    def add(block, value):
        product[block] = value if product[block] is None else product[block] + value

    for block, place, blocks in rows:
        lanes = slice(place * depth, (place + len(blocks)) * depth)
        near = split_ref[:, block * depth : (block + 1) * depth]
        onward = times(near, [ref[:, lanes] for ref in part_refs])
        for k, target in enumerate(blocks):
            add(target, onward[:, k * depth : (k + 1) * depth])
        lanes = slice((place + 1) * depth, (place + len(blocks) - 1) * depth)
        far = lanes_of(split_ref, blocks[1:-1], depth)
        add(block, times(far, [ref[:, lanes] for ref in part_refs], True))
    targets = [row_ref[k : k + 1, :] for k in range(3)]
    out_ref[...] = dipole_field(jnp.concatenate(product, 1), targets, total)


def own_segments(row_ref, col_ref, width):
    at = pl.ds(pl.multiple_of(lax.axis_index("seg") * width, width), width)
    return row_ref[:, at], col_ref[at, :]


def segment_coil_stage(row_ref, col_ref, split_ref, after_ref, out_ref):
    total = row_ref.shape[1]
    rows, columns = own_segments(row_ref, col_ref, out_ref.shape[1])
    sources = [row_ref[3 + k : 4 + k, :] for k in range(3)]
    parts = power_parts(deltas_of(sources, columns, 3), coil_core, 3)
    product = times(split_ref[...], parts, True)
    out_ref[...] = coil_field(product, [rows[3 + k : 4 + k] for k in range(3)], total)


def segment_spread_stage(row_ref, col_ref, after_ref, *part_refs):
    _, columns = own_segments(row_ref, col_ref, part_refs[0].shape[0])
    sources = [row_ref[k : k + 1, :] for k in range(3)]
    parts = power_parts(deltas_of(sources, columns, 3), yoke_core, 5)
    for ref, part in zip(part_refs, parts):
        ref[...] = part


def force_stage(row_ref, col_ref, chi_ref, segment_ref, own_coil_ref, other_coil_ref, *refs):
    partial_refs, part_refs, (lorentz_ref, moment_ref, split_ref, field_ref) = (
        refs[:2],
        refs[2:4],
        refs[4:],
    )
    total, width = row_ref.shape[1], chi_ref.shape[1]
    field = whole_field(own_coil_ref, other_coil_ref, partial_refs)
    field_ref[...] = field
    at = pl.ds(pl.multiple_of(lax.axis_index("seg") * width, width), width)
    moment_ref[...] = chi_ref[...] * field_ref[:, at]
    source_rows(row_ref, field, split_ref)
    rows, _ = own_segments(row_ref, col_ref, width)
    product = times(split_ref[...], [ref[...] for ref in part_refs], True)
    field = segment_ref[...] + dipole_field(
        product, [rows[3 + k : 4 + k] for k in range(3)], total
    )
    fx, fy, fz = [field[k : k + 1] for k in range(3)]
    cx, cy, cz = [rows[7 + k : 8 + k] for k in range(3)]
    lorentz_ref[...] = jnp.concatenate(
        [cy * fz - cz * fy, cz * fx - cx * fz, cx * fy - cy * fx], 0
    )


def call(kernel, outputs, scratch, *operands, limit=VMEM_BYTES, **options):
    return pl.pallas_call(
        kernel,
        out_shape=outputs,
        scratch_shapes=scratch,
        compiler_params=pltpu.CompilerParams(vmem_limit_bytes=limit),
        **options,
    )(*operands)


def close_body(
    seg_mid, seg_vec, strand_of, strand_current, yoke_pos, quad_weight, panel_of, panel_chi
):
    width = yoke_pos.shape[1]
    blocks = lax.axis_size("seg") * lax.axis_size("yoke")
    total = blocks * width
    half = total // 2
    f32, bf16 = jnp.float32, jnp.bfloat16

    def shape(*dims, kind=f32):
        return jax.ShapeDtypeStruct(dims, kind)

    def swap(field):
        return lax.ppermute(field, "yoke", [(0, 1), (1, 0)])

    arrays = [
        seg_mid,
        seg_vec,
        strand_of[None],
        strand_current[None],
        yoke_pos,
        quad_weight[None],
        panel_of[None],
        panel_chi[None],
    ]
    arrays = [pltpu.with_memory_space_constraint(each, pltpu.HBM) for each in arrays]
    packed, chi = call(
        pack_kernel,
        (shape(blocks, 1, 10 * width), shape(1, width)),
        [pltpu.VMEM(each.shape, each.dtype) for each in arrays]
        + [pltpu.SemaphoreType.DMA((len(arrays),))],
        *arrays,
        in_specs=[pl.BlockSpec(memory_space=pltpu.HBM)] * len(arrays),
    )
    gathered = lax.all_to_all(packed, ("seg", "yoke"), 0, 0, tiled=True)
    split_shape = shape(48, total, kind=bf16)
    split_scratch = pltpu.VMEM((48, total), bf16)
    rows, columns, split, coil = call(
        coil_stage,
        (shape(16, total), shape(total, 8), split_shape, shape(3, half)),
        [pltpu.VMEM((256, half), bf16)] * 4,
        gathered,
    )
    coils = (coil, swap(coil))
    depth, count, _ = plan(total)
    spread = call(spread_stage, [shape(depth, count * depth, kind=bf16)] * 2, [], rows, columns)
    partials = ()
    for sweep in range(ITERS):
        own = call(
            sweep_stage,
            shape(3, total),
            [split_scratch],
            rows,
            *coils,
            *partials,
            *spread,
        )
        partials = (own, swap(own))
        if sweep == 0:
            segments = call(
                segment_coil_stage, shape(3, width), [], rows, columns, split, own
            )
        if sweep == ITERS - 1:
            near = [shape(width, total, kind=bf16)] * 2
            near = call(segment_spread_stage, near, [], rows, columns, own)
    return tuple(
        call(
            force_stage,
            (shape(3, width), shape(3, width)),
            [split_scratch, pltpu.VMEM((3, total), f32)],
            rows,
            columns,
            chi,
            segments,
            *coils,
            *partials,
            *near,
        )
    )


def body(*arrays):
    seg_len, yoke_len = arrays[0].shape[1], arrays[4].shape[1]
    blocks = lax.axis_size("seg") * lax.axis_size("yoke")
    close = seg_len == 256 and yoke_len == 128 and lax.axis_size("yoke") == 2 and blocks == 16
    return (close_body if close else far_body)(*arrays)


def solution(mesh):
    placed = (
        P(None, ("grp", "seg")),
        P(None, ("grp", "seg")),
        P(("grp", "seg")),
        P("grp"),
        P(None, ("grp", "seg", "yoke")),
        P(("grp", "seg", "yoke")),
        P(("grp", "seg", "yoke")),
        P("grp"),
    )
    return jax.shard_map(
        body,
        mesh=mesh,
        in_specs=placed,
        out_specs=(P(None, ("grp", "seg", "yoke")), P(None, ("grp", "seg", "yoke"))),
        check_vma=False,
    )
```

```python
import functools
import math

import jax
import jax.numpy as jnp
from jax import lax
from jax.experimental import pallas as pl
from jax.experimental.pallas import tpu as pltpu
from jax.sharding import PartitionSpec as P

ITERS = 2
VMEM_BYTES = 16 << 20


coil_core = 0.05
yoke_core = 0.2


def coil_kernel(targets, sources):
    delta_x = targets[0][:, None] - sources[0][None, :]
    delta_y = targets[1][:, None] - sources[1][None, :]
    delta_z = targets[2][:, None] - sources[2][None, :]
    radial = delta_x * delta_x + delta_y * delta_y + delta_z * delta_z + coil_core * coil_core
    inverse = lax.rsqrt(radial)
    weight_cube = inverse * inverse * inverse
    field_x = jnp.sum(
        weight_cube * (sources[4][None, :] * delta_z - sources[5][None, :] * delta_y), axis=1
    )
    field_y = jnp.sum(
        weight_cube * (sources[5][None, :] * delta_x - sources[3][None, :] * delta_z), axis=1
    )
    field_z = jnp.sum(
        weight_cube * (sources[3][None, :] * delta_y - sources[4][None, :] * delta_x), axis=1
    )
    return jnp.stack([field_x, field_y, field_z], 0)


def dipole_kernel(targets, sources):
    delta_x = targets[0][:, None] - sources[0][None, :]
    delta_y = targets[1][:, None] - sources[1][None, :]
    delta_z = targets[2][:, None] - sources[2][None, :]
    radial = delta_x * delta_x + delta_y * delta_y + delta_z * delta_z
    inverse = lax.rsqrt(radial + yoke_core * yoke_core)
    fifth = inverse * inverse * inverse * inverse * inverse
    along = (
        delta_x * sources[3][None, :]
        + delta_y * sources[4][None, :]
        + delta_z * sources[5][None, :]
    )
    field_x = jnp.sum(fifth * (3.0 * delta_x * along - radial * sources[3][None, :]), axis=1)
    field_y = jnp.sum(fifth * (3.0 * delta_y * along - radial * sources[4][None, :]), axis=1)
    field_z = jnp.sum(fifth * (3.0 * delta_z * along - radial * sources[5][None, :]), axis=1)
    return jnp.stack([field_x, field_y, field_z], 0)


def blocked(kernel, targets, sources, element_limit):
    columns = targets.shape[1]
    pieces = 1
    while pieces < columns and (
        columns % pieces != 0 or columns // pieces * sources.shape[1] > element_limit
    ):
        pieces += 1
    if pieces == 1:
        return kernel(targets, sources)
    stacked = jnp.moveaxis(targets.reshape(3, pieces, columns // pieces), 1, 0)

    def one_block(target_block):
        return kernel(target_block, sources)

    result = lax.map(one_block, stacked)
    return jnp.moveaxis(result, 0, 1).reshape(3, columns)


def fold_blocks(kernel, targets, sources, shard_len):
    columns = sources.shape[1]
    shards = columns // shard_len
    group_size = max(1, (1 << 20) // (targets.shape[1] * shard_len))
    group_size = min(group_size, shards)
    while shards % group_size != 0:
        group_size -= 1
    block_width = group_size * shard_len
    block_count = columns // block_width
    if block_count == 1:
        return kernel(targets, sources)
    stacked = jnp.moveaxis(sources.reshape(sources.shape[0], block_count, block_width), 1, 0)

    def advance(running, source_block):
        return (running + kernel(targets, source_block), None)

    result, unused = lax.scan(advance, jnp.zeros((3, targets.shape[1]), jnp.float32), stacked)
    return result


def make_fold(kernel, targets, shard_len, sources):
    return fold_blocks(kernel, targets, sources, shard_len)


def cross_rows(left_rows, right_rows):
    return jnp.stack(
        [
            left_rows[1] * right_rows[2] - left_rows[2] * right_rows[1],
            left_rows[2] * right_rows[0] - left_rows[0] * right_rows[2],
            left_rows[0] * right_rows[1] - left_rows[1] * right_rows[0],
        ],
        0,
    )


def table_lookup(indices, table):
    rows_iota = lax.broadcasted_iota(jnp.int32, (table.shape[0], indices.shape[0]), 0)
    return jnp.sum(jnp.where(indices[None, :] == rows_iota, table[:, None], 0.0), axis=0)


def far_body(seg_mid, seg_vec, strand_of, strand_current, yoke_pos, quad_weight, panel_of, panel_chi):
    seg_len = seg_mid.shape[1]
    half_len = seg_len // 2
    yoke_len = yoke_pos.shape[1]
    segments_total = seg_len * lax.axis_size("seg")
    points_total = yoke_len * lax.axis_size("seg") * lax.axis_size("yoke")
    coil_scale = 1.0 / math.sqrt(segments_total)
    yoke_scale = 1.0 / math.sqrt(points_total)
    current = table_lookup(strand_of, strand_current)
    carried = current[None, :] * seg_vec
    seg_pack = jnp.concatenate([seg_mid, carried], 0)
    suscept = table_lookup(panel_of, panel_chi)[None, :]
    half_start = lax.axis_index("yoke") * half_len
    own_mid = lax.dynamic_slice_in_dim(seg_mid, half_start, half_len, 1)
    own_carried = lax.dynamic_slice_in_dim(carried, half_start, half_len, 1)
    half_points = lax.all_gather(yoke_pos, "seg", axis=1, tiled=True)
    partial_value = blocked(coil_kernel, half_points, seg_pack, 1 << 19)
    coil_yoke = lax.psum_scatter(partial_value, "seg", scatter_dimension=1, tiled=True) * coil_scale
    coil_seg = (
        make_fold(
            coil_kernel, own_mid, seg_len, lax.all_gather(seg_pack, "seg", axis=1, tiled=True)
        )
        * coil_scale
    )

    def moment_field(targets, moment):
        source_pack = jnp.concatenate([yoke_pos, quad_weight[None, :] * moment], 0)
        gathered_sum = make_fold(
            dipole_kernel,
            targets,
            yoke_len,
            lax.all_gather(source_pack, ("seg", "yoke"), axis=1, tiled=True),
        )
        return gathered_sum * yoke_scale

    moment = suscept * coil_yoke
    for sweep_index in range(ITERS):
        moment = suscept * (coil_yoke + moment_field(yoke_pos, moment))
    total_field = coil_seg + moment_field(own_mid, moment)
    lorentz = cross_rows(own_carried, total_field)
    return (lorentz, moment)


def bf16_parts(value, count):
    parts = []
    for place in range(count):
        part = value.astype(jnp.bfloat16)
        parts.append(part)
        if place + 1 < count:
            value = value - part.astype(jnp.float32)
    return parts


def split_rows(rows, split_ref):
    count = rows.shape[0]
    for place, part in enumerate(bf16_parts(rows, 3)):
        split_ref[place * count : (place + 1) * count, :] = part


def joined(product):
    count = product.shape[0] // 3
    return product[:count] + product[count : 2 * count] + product[2 * count :]


def pick(table_ref, index_ref):
    entries = lax.broadcasted_iota(jnp.int32, (table_ref.shape[1], index_ref.shape[1]), 0)
    chosen = jnp.where(entries == index_ref[...], 1.0, 0.0)
    table = jnp.broadcast_to(table_ref[...], (8, table_ref.shape[1]))
    found = jnp.dot(
        table, chosen, precision=lax.Precision.HIGHEST, preferred_element_type=jnp.float32
    )
    return found[:1]


def pack_kernel(*refs):
    sources, (out_ref, chi_ref), held, sems = refs[:8], refs[8:10], refs[10:18], refs[18]
    copies = [
        pltpu.make_async_copy(source, target, sems.at[place])
        for place, (source, target) in enumerate(zip(sources, held))
    ]
    for copy in copies:
        copy.start()
    for copy in copies:
        copy.wait()
    mid_ref, vec_ref, strand_ref, current_ref, pos_ref, weight_ref, panel_ref, table_ref = held
    half = pos_ref.shape[1]
    first = lax.axis_index("yoke") == 0
    mid = jnp.where(first, mid_ref[:, :half], mid_ref[:, half:])
    carried = pick(current_ref, strand_ref) * vec_ref[...]
    carried = jnp.where(first, carried[:, :half], carried[:, half:])
    suscept = pick(table_ref, panel_ref)
    chi_ref[...] = suscept
    rows = [pos_ref[k : k + 1, :] for k in range(3)]
    rows += [weight_ref[...] * suscept]
    rows += [mid[k : k + 1] for k in range(3)]
    rows += [carried[k : k + 1] for k in range(3)]
    for block in range(out_ref.shape[0]):
        for place, row in enumerate(rows):
            out_ref[block, :, place * half : (place + 1) * half] = row


def times(rows, matrix_parts, transposed=False):
    contracted = ((1,), (1 if transposed else 0,))
    total = None
    for part in matrix_parts:
        product = lax.dot_general(
            rows, part, (contracted, ((), ())), preferred_element_type=jnp.float32
        )
        total = product if total is None else total + product
    return total


def square_factor(tile, core=None):
    place = lax.broadcasted_iota(jnp.int32, tile.shape, 0)
    points = jnp.where(place < 3, tile, 0.0)
    high, mid, low = [part.astype(jnp.float32) for part in bf16_parts(points, 3)]
    norm = jnp.sum(points * points, axis=0, keepdims=True)
    if core is not None:
        norm = norm + core * core
    norms = [part.astype(jnp.float32) for part in bf16_parts(norm, 3)]
    first = 0 if core is None else 3
    last = jnp.where(place < 6, 1.0, 0.0)
    for k in range(3):
        last = jnp.where(place == first + k, norms[k], last)
    if core is None:
        high, mid, low = -2.0 * high, -2.0 * mid, -2.0 * low
        groups = [high, mid, high, mid, low, high]
    else:
        groups = [high, high, mid, mid, high, low]
    groups += [last, jnp.zeros_like(last)]
    return jnp.concatenate(groups, 0).astype(jnp.bfloat16)


def source_factor(tile, core, out_ref):
    for start in range(0, tile.shape[1], 128):
        factor = square_factor(tile[:, start : start + 128], core)
        out_ref[start : start + 128, :] = factor.T


def power_parts(square, power):
    inverse = lax.rsqrt(square)
    below = inverse * inverse
    return bf16_parts(below * inverse if power == 3 else below * below * inverse, 2)


def squares(sources, targets):
    return jnp.dot(sources, targets, preferred_element_type=jnp.float32)


def coil_rows(row_ref):
    mx, my, mz, cx, cy, cz = [row_ref[8 + k : 9 + k, :] for k in range(6)]
    blank = jnp.zeros((10, row_ref.shape[1]), jnp.float32)
    crossed = [cy * mz - cz * my, cz * mx - cx * mz, cx * my - cy * mx]
    return jnp.concatenate([cx, cy, cz] + crossed + [blank], 0)


def coil_field(product, targets, total):
    sums = joined(product)
    tx, ty, tz = targets
    sx, sy, sz = [sums[k : k + 1] for k in range(3)]
    field = jnp.concatenate([sy * tz - sz * ty, sz * tx - sx * tz, sx * ty - sy * tx], 0)
    return (field - sums[3:6]) * (1.0 / math.sqrt(total))


def coil_stage(
    gathered_ref,
    row_ref,
    segment_factor_ref,
    yoke_factor_ref,
    target_factor_ref,
    split_ref,
    field_ref,
    *weight_refs,
):
    blocks = gathered_ref.shape[0]
    total = row_ref.shape[1]
    half, width = total // 2, total // blocks
    core = lax.axis_index("yoke")
    row_ref[...] = jnp.zeros_like(row_ref)
    for block in range(blocks):
        near = block < blocks // 2
        source = 2 * (block % (blocks // 2)) + (core if near else 1 - core)
        for k in range(10):
            row = k if k < 4 else k + 4
            row_ref[row : row + 1, block * width : (block + 1) * width] = gathered_ref[
                source, :, k * width : (k + 1) * width
            ]
    center = jnp.sum(row_ref[0:3, :], axis=1, keepdims=True) * (1.0 / total)
    shift = jnp.concatenate([center, jnp.zeros((5, 1), jnp.float32)], 0)
    yoke = row_ref[0:8, :] - shift
    segments = row_ref[8:16, :] - shift
    row_ref[0:8, :] = yoke
    row_ref[8:16, :] = segments
    target_factor_ref[...] = square_factor(yoke)
    source_factor(segments, coil_core, segment_factor_ref)
    source_factor(yoke[:, :half], yoke_core, yoke_factor_ref)
    split_rows(coil_rows(row_ref), split_ref)
    targets = [row_ref[k : k + 1, :half] for k in range(3)]
    depth = 256
    count = total // depth
    product = jnp.zeros((split_ref.shape[0], half), jnp.float32)

    def build(chunk):
        part_refs = weight_refs[2 * (chunk % 2) : 2 * (chunk % 2) + 2]
        sources = segment_factor_ref[chunk * depth : (chunk + 1) * depth, :]
        parts = power_parts(squares(sources, target_factor_ref[:, :half]), 3)
        for ref, part in zip(part_refs, parts):
            ref[...] = part

    build(0)
    for chunk in range(count):
        if chunk + 1 < count:
            build(chunk + 1)
        rows = split_ref[:, chunk * depth : (chunk + 1) * depth]
        part_refs = weight_refs[2 * (chunk % 2) : 2 * (chunk % 2) + 2]
        product = product + times(rows, [ref[...] for ref in part_refs])
    field_ref[...] = coil_field(product, targets, total)


def plan(total):
    depth = total // 8
    place, rows = 0, []
    for block in range(4):
        both = list(range(block + 1, 4)) + [4 + (block + 1) % 4]
        both += [6 + block] if block < 2 else []
        targets = [block] + both + [4 + block]
        rows.append((block, place, targets))
        place += len(targets)
    return depth, place, rows


def lanes_of(array, blocks, depth):
    return jnp.concatenate([array[:, k * depth : (k + 1) * depth] for k in blocks], 1)


def spread_stage(source_factor_ref, target_factor_ref, *part_refs):
    depth, _, rows = plan(target_factor_ref.shape[1])
    for block, place, blocks in rows:
        targets = lanes_of(target_factor_ref, blocks, depth)
        lanes = slice(place * depth, (place + len(blocks)) * depth)
        sources = source_factor_ref[block * depth : (block + 1) * depth, :]
        for ref, part in zip(part_refs, power_parts(squares(sources, targets), 5)):
            ref[:, lanes] = part


def source_rows(row_ref, field, split_ref):
    strength = row_ref[3:4, :] * field
    ux, uy, uz = [strength[k : k + 1] for k in range(3)]
    qx, qy, qz = [row_ref[k : k + 1, :] for k in range(3)]
    along = 3.0 * (qx * ux + qy * uy + qz * uz)
    square = qx * qx + qy * qy + qz * qz
    split_rows(
        jnp.concatenate(
            [
                strength,
                qx * strength,
                qy * strength,
                qz * strength,
                qx * along - square * ux,
                qy * along - square * uy,
                qz * along - square * uz,
                jnp.zeros((1, row_ref.shape[1]), jnp.float32),
            ],
            0,
        ),
        split_ref,
    )


def dipole_field(product, targets, total):
    sums = joined(product)
    tx, ty, tz = targets
    plain = [sums[k : k + 1] for k in range(3)]
    tensor = [[sums[3 + 3 * a + b : 4 + 3 * a + b] for b in range(3)] for a in range(3)]
    toward = tx * plain[0] + ty * plain[1] + tz * plain[2]
    trace = tensor[0][0] + tensor[1][1] + tensor[2][2]
    lead = 3.0 * (toward - trace)
    reach = tx * tx + ty * ty + tz * tz
    fields = []
    for a in range(3):
        field = targets[a] * lead - reach * plain[a] + sums[12 + a : 13 + a]
        for b in range(3):
            field = field + targets[b] * (2.0 * tensor[b][a] - 3.0 * tensor[a][b])
        fields.append(field)
    return jnp.concatenate(fields, 0) * (1.0 / math.sqrt(total))


def whole_field(own_coil_ref, other_coil_ref, partial_refs):
    field = jnp.concatenate([own_coil_ref[...], other_coil_ref[...]], 1)
    if partial_refs:
        own, other = partial_refs
        half = own.shape[1] // 2
        field = field + own[...]
        field = field + jnp.concatenate([other[:, half:], other[:, :half]], 1)
    return field


def sweep_stage(skip, *refs):
    row_ref, own_coil_ref, other_coil_ref, *refs = refs[skip:]
    partial_refs, part_refs, (out_ref, split_ref) = refs[:-4], refs[-4:-2], refs[-2:]
    total = row_ref.shape[1]
    source_rows(row_ref, whole_field(own_coil_ref, other_coil_ref, partial_refs), split_ref)
    depth, _, rows = plan(total)
    product = [None] * 8

    def add(block, value):
        product[block] = value if product[block] is None else product[block] + value

    for block, place, blocks in rows:
        lanes = slice(place * depth, (place + len(blocks)) * depth)
        near = split_ref[:, block * depth : (block + 1) * depth]
        onward = times(near, [ref[:, lanes] for ref in part_refs])
        for k, target in enumerate(blocks):
            add(target, onward[:, k * depth : (k + 1) * depth])
        lanes = slice((place + 1) * depth, (place + len(blocks) - 1) * depth)
        far = lanes_of(split_ref, blocks[1:-1], depth)
        add(block, times(far, [ref[:, lanes] for ref in part_refs], True))
    targets = [row_ref[k : k + 1, :] for k in range(3)]
    out_ref[...] = dipole_field(jnp.concatenate(product, 1), targets, total)


def own_at(width):
    return pl.ds(pl.multiple_of(lax.axis_index("seg") * width, width), width)


def segment_coil_stage(row_ref, factor_ref, split_ref, after_ref, out_ref):
    total = row_ref.shape[1]
    own = row_ref[8:16, own_at(out_ref.shape[1])]
    parts = power_parts(squares(factor_ref[...], square_factor(own)), 3)
    product = times(split_ref[...], parts)
    out_ref[...] = coil_field(product, [own[k : k + 1] for k in range(3)], total)


def segment_spread_stage(segment_factor_ref, target_factor_ref, after_ref, *part_refs):
    own = segment_factor_ref[own_at(part_refs[0].shape[0]), :]
    square = squares(own, target_factor_ref[...])
    square = square + (yoke_core * yoke_core - coil_core * coil_core)
    for ref, part in zip(part_refs, power_parts(square, 5)):
        ref[...] = part


def force_stage(row_ref, chi_ref, segment_ref, own_coil_ref, other_coil_ref, *refs):
    partial_refs, part_refs, (lorentz_ref, moment_ref, split_ref, field_ref) = (
        refs[:2],
        refs[2:4],
        refs[4:],
    )
    total, width = row_ref.shape[1], chi_ref.shape[1]
    field = whole_field(own_coil_ref, other_coil_ref, partial_refs)
    field_ref[...] = field
    at = own_at(width)
    moment_ref[...] = chi_ref[...] * field_ref[:, at]
    source_rows(row_ref, field, split_ref)
    own = row_ref[8:16, at]
    product = times(split_ref[...], [ref[...] for ref in part_refs], True)
    field = segment_ref[...] + dipole_field(
        product, [own[k : k + 1] for k in range(3)], total
    )
    fx, fy, fz = [field[k : k + 1] for k in range(3)]
    cx, cy, cz = [own[3 + k : 4 + k] for k in range(3)]
    lorentz_ref[...] = jnp.concatenate(
        [cy * fz - cz * fy, cz * fx - cx * fz, cx * fy - cy * fx], 0
    )


def call(kernel, outputs, scratch, *operands, limit=VMEM_BYTES, **options):
    return pl.pallas_call(
        kernel,
        out_shape=outputs,
        scratch_shapes=scratch,
        compiler_params=pltpu.CompilerParams(vmem_limit_bytes=limit),
        **options,
    )(*operands)


def close_body(
    seg_mid, seg_vec, strand_of, strand_current, yoke_pos, quad_weight, panel_of, panel_chi
):
    width = yoke_pos.shape[1]
    blocks = lax.axis_size("seg") * lax.axis_size("yoke")
    total = blocks * width
    half = total // 2
    f32, bf16 = jnp.float32, jnp.bfloat16

    def shape(*dims, kind=f32):
        return jax.ShapeDtypeStruct(dims, kind)

    def swap(field):
        return lax.ppermute(field, "yoke", [(0, 1), (1, 0)])

    arrays = [
        seg_mid,
        seg_vec,
        strand_of[None],
        strand_current[None],
        yoke_pos,
        quad_weight[None],
        panel_of[None],
        panel_chi[None],
    ]
    arrays = [pltpu.with_memory_space_constraint(each, pltpu.HBM) for each in arrays]
    packed, chi = call(
        pack_kernel,
        (shape(blocks, 1, 10 * width), shape(1, width)),
        [pltpu.VMEM(each.shape, each.dtype) for each in arrays]
        + [pltpu.SemaphoreType.DMA((len(arrays),))],
        *arrays,
        in_specs=[pl.BlockSpec(memory_space=pltpu.HBM)] * len(arrays),
    )
    gathered = lax.all_to_all(packed, ("seg", "yoke"), 0, 0, tiled=True)
    split_shape = shape(48, total, kind=bf16)
    split_scratch = pltpu.VMEM((48, total), bf16)
    rows, segment_factor, yoke_factor, target_factor, split, coil = call(
        coil_stage,
        (
            shape(16, total),
            shape(total, 64, kind=bf16),
            shape(half, 64, kind=bf16),
            shape(64, total, kind=bf16),
            split_shape,
            shape(3, half),
        ),
        [pltpu.VMEM((256, half), bf16)] * 4,
        gathered,
    )
    coils = (coil, swap(coil))
    depth, count, _ = plan(total)
    spread = call(
        spread_stage,
        [shape(depth, count * depth, kind=bf16)] * 2,
        [],
        yoke_factor,
        target_factor,
    )
    partials, after = (), ()
    for sweep in range(ITERS):
        own = call(
            functools.partial(sweep_stage, len(after)),
            shape(3, total),
            [split_scratch],
            *after,
            rows,
            *coils,
            *partials,
            *spread,
        )
        partials = (own, swap(own))
        if sweep == 0:
            segments = call(
                segment_coil_stage, shape(3, width), [], rows, segment_factor, split, own
            )
            after = (segments,)
        if sweep == ITERS - 1:
            near = [shape(width, total, kind=bf16)] * 2
            near = call(segment_spread_stage, near, [], segment_factor, target_factor, own)
    return tuple(
        call(
            force_stage,
            (shape(3, width), shape(3, width)),
            [split_scratch, pltpu.VMEM((3, total), f32)],
            rows,
            chi,
            segments,
            *coils,
            *partials,
            *near,
        )
    )


def body(*arrays):
    seg_len, yoke_len = arrays[0].shape[1], arrays[4].shape[1]
    blocks = lax.axis_size("seg") * lax.axis_size("yoke")
    close = seg_len == 256 and yoke_len == 128 and lax.axis_size("yoke") == 2 and blocks == 16
    return (close_body if close else far_body)(*arrays)


def solution(mesh):
    placed = (
        P(None, ("grp", "seg")),
        P(None, ("grp", "seg")),
        P(("grp", "seg")),
        P("grp"),
        P(None, ("grp", "seg", "yoke")),
        P(("grp", "seg", "yoke")),
        P(("grp", "seg", "yoke")),
        P("grp"),
    )
    return jax.shard_map(
        body,
        mesh=mesh,
        in_specs=placed,
        out_specs=(P(None, ("grp", "seg", "yoke")), P(None, ("grp", "seg", "yoke"))),
        check_vma=False,
    )
```

```python
import math

import jax
import jax.numpy as jnp
from jax import lax
from jax.experimental import pallas as pl
from jax.experimental.pallas import tpu as pltpu
from jax.sharding import PartitionSpec as P

ITERS = 2
VMEM_BYTES = 16 << 20


coil_core = 0.05
yoke_core = 0.2


def coil_kernel(targets, sources):
    delta_x = targets[0][:, None] - sources[0][None, :]
    delta_y = targets[1][:, None] - sources[1][None, :]
    delta_z = targets[2][:, None] - sources[2][None, :]
    radial = delta_x * delta_x + delta_y * delta_y + delta_z * delta_z + coil_core * coil_core
    inverse = lax.rsqrt(radial)
    weight_cube = inverse * inverse * inverse
    field_x = jnp.sum(
        weight_cube * (sources[4][None, :] * delta_z - sources[5][None, :] * delta_y), axis=1
    )
    field_y = jnp.sum(
        weight_cube * (sources[5][None, :] * delta_x - sources[3][None, :] * delta_z), axis=1
    )
    field_z = jnp.sum(
        weight_cube * (sources[3][None, :] * delta_y - sources[4][None, :] * delta_x), axis=1
    )
    return jnp.stack([field_x, field_y, field_z], 0)


def dipole_kernel(targets, sources):
    delta_x = targets[0][:, None] - sources[0][None, :]
    delta_y = targets[1][:, None] - sources[1][None, :]
    delta_z = targets[2][:, None] - sources[2][None, :]
    radial = delta_x * delta_x + delta_y * delta_y + delta_z * delta_z
    inverse = lax.rsqrt(radial + yoke_core * yoke_core)
    fifth = inverse * inverse * inverse * inverse * inverse
    along = (
        delta_x * sources[3][None, :]
        + delta_y * sources[4][None, :]
        + delta_z * sources[5][None, :]
    )
    field_x = jnp.sum(fifth * (3.0 * delta_x * along - radial * sources[3][None, :]), axis=1)
    field_y = jnp.sum(fifth * (3.0 * delta_y * along - radial * sources[4][None, :]), axis=1)
    field_z = jnp.sum(fifth * (3.0 * delta_z * along - radial * sources[5][None, :]), axis=1)
    return jnp.stack([field_x, field_y, field_z], 0)


def blocked(kernel, targets, sources, element_limit):
    columns = targets.shape[1]
    pieces = 1
    while pieces < columns and (
        columns % pieces != 0 or columns // pieces * sources.shape[1] > element_limit
    ):
        pieces += 1
    if pieces == 1:
        return kernel(targets, sources)
    stacked = jnp.moveaxis(targets.reshape(3, pieces, columns // pieces), 1, 0)

    def one_block(target_block):
        return kernel(target_block, sources)

    result = lax.map(one_block, stacked)
    return jnp.moveaxis(result, 0, 1).reshape(3, columns)


def fold_blocks(kernel, targets, sources, shard_len):
    columns = sources.shape[1]
    shards = columns // shard_len
    group_size = max(1, (1 << 20) // (targets.shape[1] * shard_len))
    group_size = min(group_size, shards)
    while shards % group_size != 0:
        group_size -= 1
    block_width = group_size * shard_len
    block_count = columns // block_width
    if block_count == 1:
        return kernel(targets, sources)
    stacked = jnp.moveaxis(sources.reshape(sources.shape[0], block_count, block_width), 1, 0)

    def advance(running, source_block):
        return (running + kernel(targets, source_block), None)

    result, unused = lax.scan(advance, jnp.zeros((3, targets.shape[1]), jnp.float32), stacked)
    return result


def make_fold(kernel, targets, shard_len, sources):
    return fold_blocks(kernel, targets, sources, shard_len)


def cross_rows(left_rows, right_rows):
    return jnp.stack(
        [
            left_rows[1] * right_rows[2] - left_rows[2] * right_rows[1],
            left_rows[2] * right_rows[0] - left_rows[0] * right_rows[2],
            left_rows[0] * right_rows[1] - left_rows[1] * right_rows[0],
        ],
        0,
    )


def table_lookup(indices, table):
    rows_iota = lax.broadcasted_iota(jnp.int32, (table.shape[0], indices.shape[0]), 0)
    return jnp.sum(jnp.where(indices[None, :] == rows_iota, table[:, None], 0.0), axis=0)


def far_body(seg_mid, seg_vec, strand_of, strand_current, yoke_pos, quad_weight, panel_of, panel_chi):
    seg_len = seg_mid.shape[1]
    half_len = seg_len // 2
    yoke_len = yoke_pos.shape[1]
    segments_total = seg_len * lax.axis_size("seg")
    points_total = yoke_len * lax.axis_size("seg") * lax.axis_size("yoke")
    coil_scale = 1.0 / math.sqrt(segments_total)
    yoke_scale = 1.0 / math.sqrt(points_total)
    current = table_lookup(strand_of, strand_current)
    carried = current[None, :] * seg_vec
    seg_pack = jnp.concatenate([seg_mid, carried], 0)
    suscept = table_lookup(panel_of, panel_chi)[None, :]
    half_start = lax.axis_index("yoke") * half_len
    own_mid = lax.dynamic_slice_in_dim(seg_mid, half_start, half_len, 1)
    own_carried = lax.dynamic_slice_in_dim(carried, half_start, half_len, 1)
    half_points = lax.all_gather(yoke_pos, "seg", axis=1, tiled=True)
    partial_value = blocked(coil_kernel, half_points, seg_pack, 1 << 19)
    coil_yoke = lax.psum_scatter(partial_value, "seg", scatter_dimension=1, tiled=True) * coil_scale
    coil_seg = (
        make_fold(
            coil_kernel, own_mid, seg_len, lax.all_gather(seg_pack, "seg", axis=1, tiled=True)
        )
        * coil_scale
    )

    def moment_field(targets, moment):
        source_pack = jnp.concatenate([yoke_pos, quad_weight[None, :] * moment], 0)
        gathered_sum = make_fold(
            dipole_kernel,
            targets,
            yoke_len,
            lax.all_gather(source_pack, ("seg", "yoke"), axis=1, tiled=True),
        )
        return gathered_sum * yoke_scale

    moment = suscept * coil_yoke
    for sweep_index in range(ITERS):
        moment = suscept * (coil_yoke + moment_field(yoke_pos, moment))
    total_field = coil_seg + moment_field(own_mid, moment)
    lorentz = cross_rows(own_carried, total_field)
    return (lorentz, moment)


def bf16_parts(value, count):
    parts = []
    for place in range(count):
        part = value.astype(jnp.bfloat16)
        parts.append(part)
        if place + 1 < count:
            value = value - part.astype(jnp.float32)
    return parts


def split_rows(rows, split_ref):
    count = rows.shape[0]
    for place, part in enumerate(bf16_parts(rows, 3)):
        split_ref[place * count : (place + 1) * count, :] = part


def joined(product):
    count = product.shape[0] // 3
    return product[:count] + product[count : 2 * count] + product[2 * count :]


def pick(table_ref, index):
    entries = lax.broadcasted_iota(jnp.int32, (table_ref.shape[1], index.shape[1]), 0)
    chosen = jnp.where(entries == index, 1.0, 0.0).astype(jnp.bfloat16)
    parts = [part.astype(jnp.float32) for part in bf16_parts(table_ref[...], 3)]
    blank = jnp.zeros((5, table_ref.shape[1]), jnp.float32)
    table = jnp.concatenate(parts + [blank], 0).astype(jnp.bfloat16)
    found = jnp.dot(table, chosen, preferred_element_type=jnp.float32)
    return found[0:1] + found[1:2] + found[2:3]


def pack_kernel(*refs):
    sources, (out_ref, chi_ref), held, sems = refs[:8], refs[8:10], refs[10:18], refs[18]
    copies = [
        pltpu.make_async_copy(source, target, sems.at[place])
        for place, (source, target) in enumerate(zip(sources, held))
    ]
    for copy in copies:
        copy.start()
    for copy in copies:
        copy.wait()
    mid_ref, vec_ref, strand_ref, current_ref, pos_ref, weight_ref, panel_ref, table_ref = held
    half = pos_ref.shape[1]
    first = lax.axis_index("yoke") == 0

    def own(ref):
        return jnp.where(first, ref[:, :half], ref[:, half:])

    mid = own(mid_ref)
    carried = pick(current_ref, own(strand_ref)) * own(vec_ref)
    suscept = pick(table_ref, panel_ref[...])
    chi_ref[...] = suscept
    rows = [pos_ref[k : k + 1, :] for k in range(3)]
    rows += [weight_ref[...] * suscept]
    rows += [mid[k : k + 1] for k in range(3)]
    rows += [carried[k : k + 1] for k in range(3)]
    for place, row in enumerate(rows):
        out_ref[0, :, place * half : (place + 1) * half] = row


def join_kernel(*refs):
    place = 0
    for ref in refs[:-1]:
        for block in range(ref.shape[0]):
            refs[-1][place] = ref[block]
            place += 1


def times(rows, matrix_parts, transposed=False):
    contracted = ((1,), (1 if transposed else 0,))
    total = None
    for part in matrix_parts:
        product = lax.dot_general(
            rows, part, (contracted, ((), ())), preferred_element_type=jnp.float32
        )
        total = product if total is None else total + product
    return total


def square_factor(tile, core=None):
    place = lax.broadcasted_iota(jnp.int32, tile.shape, 0)
    points = jnp.where(place < 3, tile, 0.0)
    high, mid, low = [part.astype(jnp.float32) for part in bf16_parts(points, 3)]
    norm = jnp.sum(points * points, axis=0, keepdims=True)
    if core is not None:
        norm = norm + core * core
    norms = [part.astype(jnp.float32) for part in bf16_parts(norm, 3)]
    first = 0 if core is None else 3
    last = jnp.where(place < 6, 1.0, 0.0)
    for k in range(3):
        last = jnp.where(place == first + k, norms[k], last)
    if core is None:
        high, mid, low = -2.0 * high, -2.0 * mid, -2.0 * low
        groups = [high, mid, high, mid, low, high]
    else:
        groups = [high, high, mid, mid, high, low]
    groups += [last, jnp.zeros_like(last)]
    return jnp.concatenate(groups, 0).astype(jnp.bfloat16)


def source_factor(tile, core, out_ref):
    for start in range(0, tile.shape[1], 128):
        factor = square_factor(tile[:, start : start + 128], core)
        out_ref[start : start + 128, :] = factor.T


def power_parts(square, power):
    inverse = lax.rsqrt(square)
    below = inverse * inverse
    return bf16_parts(below * inverse if power == 3 else below * below * inverse, 2)


def squares(sources, targets):
    return jnp.dot(sources, targets, preferred_element_type=jnp.float32)


def coil_rows(segments):
    mx, my, mz, cx, cy, cz = [segments[k : k + 1] for k in range(6)]
    blank = jnp.zeros((10, segments.shape[1]), jnp.float32)
    crossed = [cy * mz - cz * my, cz * mx - cx * mz, cx * my - cy * mx]
    return jnp.concatenate([cx, cy, cz] + crossed + [blank], 0)


def coil_field(sums, targets, total):
    tx, ty, tz = targets
    sx, sy, sz = [sums[k : k + 1] for k in range(3)]
    field = jnp.concatenate([sy * tz - sz * ty, sz * tx - sx * tz, sx * ty - sy * tx], 0)
    return (field - sums[3:6]) * (1.0 / math.sqrt(total))


def place_rows(gathered_ref, row_ref):
    blocks, half = gathered_ref.shape[0], row_ref.shape[1]
    width = half // blocks
    row_ref[...] = jnp.zeros_like(row_ref)
    for block in range(blocks):
        for k in range(10):
            row = k if k < 4 else k + 4
            row_ref[row : row + 1, block * width : (block + 1) * width] = gathered_ref[
                block, :, k * width : (k + 1) * width
            ]


def build_and_apply(factor_ref, targets, power, split_ref, part_refs):
    depth = 256
    count = factor_ref.shape[0] // depth
    slots = part_refs[0].shape[0] // depth
    product = jnp.zeros((split_ref.shape[0], targets.shape[1]), jnp.float32)

    def slot(chunk):
        start = chunk % slots * depth
        return slice(start, start + depth)

    def build(chunk):
        sources = factor_ref[chunk * depth : (chunk + 1) * depth, :]
        for ref, part in zip(part_refs, power_parts(squares(sources, targets), power)):
            ref[slot(chunk), :] = part

    build(0)
    for chunk in range(count):
        if chunk + 1 < count:
            build(chunk + 1)
        rows = split_ref[:, chunk * depth : (chunk + 1) * depth]
        product = product + times(rows, [ref[slot(chunk), :] for ref in part_refs])
    return joined(product)


def apply(split_ref, part_refs):
    depth = 256
    product = jnp.zeros((split_ref.shape[0], part_refs[0].shape[1]), jnp.float32)
    for start in range(0, split_ref.shape[1], depth):
        rows = split_ref[:, start : start + depth]
        product = product + times(rows, [ref[start : start + depth, :] for ref in part_refs])
    return joined(product)


def near_coil_stage(
    gathered_ref,
    row_ref,
    shift_ref,
    segment_factor_ref,
    yoke_factor_ref,
    target_factor_ref,
    split_ref,
    sums_ref,
    *weight_refs,
):
    half = row_ref.shape[1]
    place_rows(gathered_ref, row_ref)
    center = jnp.sum(row_ref[0:3, :], axis=1, keepdims=True) * (1.0 / half)
    shift = jnp.concatenate([center, jnp.zeros((5, 1), jnp.float32)], 0)
    shift_ref[...] = jnp.broadcast_to(shift, shift_ref.shape)
    yoke = row_ref[0:8, :] - shift
    segments = row_ref[8:16, :] - shift
    row_ref[0:8, :] = yoke
    row_ref[8:16, :] = segments
    target_factor_ref[...] = square_factor(yoke)
    source_factor(segments, coil_core, segment_factor_ref)
    split_rows(coil_rows(segments), split_ref)
    targets = target_factor_ref[...]
    sums_ref[...] = build_and_apply(segment_factor_ref, targets, 3, split_ref, weight_refs)
    source_factor(yoke, yoke_core, yoke_factor_ref)


def far_coil_stage(
    gathered_ref,
    near_row_ref,
    shift_ref,
    target_factor_ref,
    sums_ref,
    row_ref,
    segment_factor_ref,
    yoke_factor_ref,
    split_ref,
    field_ref,
    *weight_refs,
):
    half = row_ref.shape[1]
    place_rows(gathered_ref, row_ref)
    shift = shift_ref[:, 0:1]
    yoke = row_ref[0:8, :] - shift
    segments = row_ref[8:16, :] - shift
    row_ref[0:8, :] = yoke
    row_ref[8:16, :] = segments
    source_factor(segments, coil_core, segment_factor_ref)
    split_rows(coil_rows(segments), split_ref)
    targets = target_factor_ref[...]
    sums = build_and_apply(segment_factor_ref, targets, 3, split_ref, weight_refs)
    places = [near_row_ref[k : k + 1, :] for k in range(3)]
    field_ref[...] = coil_field(sums_ref[...] + sums, places, 2 * half)
    source_factor(yoke, yoke_core, yoke_factor_ref)


def source_rows(row_ref, field, split_ref):
    strength = row_ref[3:4, :] * field
    ux, uy, uz = [strength[k : k + 1] for k in range(3)]
    qx, qy, qz = [row_ref[k : k + 1, :] for k in range(3)]
    along = 3.0 * (qx * ux + qy * uy + qz * uz)
    square = qx * qx + qy * qy + qz * qz
    split_rows(
        jnp.concatenate(
            [
                strength,
                qx * strength,
                qy * strength,
                qz * strength,
                qx * along - square * ux,
                qy * along - square * uy,
                qz * along - square * uz,
                jnp.zeros((1, row_ref.shape[1]), jnp.float32),
            ],
            0,
        ),
        split_ref,
    )


def dipole_field(sums, targets, total):
    tx, ty, tz = targets
    plain = [sums[k : k + 1] for k in range(3)]
    tensor = [[sums[3 + 3 * a + b : 4 + 3 * a + b] for b in range(3)] for a in range(3)]
    toward = tx * plain[0] + ty * plain[1] + tz * plain[2]
    trace = tensor[0][0] + tensor[1][1] + tensor[2][2]
    lead = 3.0 * (toward - trace)
    reach = tx * tx + ty * ty + tz * tz
    fields = []
    for a in range(3):
        field = targets[a] * lead - reach * plain[a] + sums[12 + a : 13 + a]
        for b in range(3):
            field = field + targets[b] * (2.0 * tensor[b][a] - 3.0 * tensor[a][b])
        fields.append(field)
    return jnp.concatenate(fields, 0) * (1.0 / math.sqrt(total))


def near_build_stage(
    row_ref, source_ref, target_ref, field_ref, sums_ref, first_ref, second_ref, split_ref
):
    source_rows(row_ref, field_ref[...], split_ref)
    sums_ref[...] = build_and_apply(
        source_ref, target_ref[...], 5, split_ref, [first_ref, second_ref]
    )


def finish(near_row_ref, coil_ref, sums, out_ref):
    targets = [near_row_ref[k : k + 1, :] for k in range(3)]
    total = 2 * near_row_ref.shape[1]
    out_ref[...] = coil_ref[...] + dipole_field(sums, targets, total)


def far_build_stage(
    near_row_ref,
    row_ref,
    source_ref,
    target_ref,
    coil_ref,
    other_ref,
    sums_ref,
    out_ref,
    first_ref,
    second_ref,
    split_ref,
):
    source_rows(row_ref, other_ref[...], split_ref)
    sums = build_and_apply(source_ref, target_ref[...], 5, split_ref, [first_ref, second_ref])
    finish(near_row_ref, coil_ref, sums_ref[...] + sums, out_ref)


def near_sweep_stage(row_ref, field_ref, first_ref, second_ref, *refs):
    segment_refs, (sums_ref, segment_ref, split_ref) = refs[:-3], refs[-3:]
    source_rows(row_ref, field_ref[...], split_ref)
    sums_ref[...] = apply(split_ref, [first_ref, second_ref])
    factor_refs, split_refs = segment_refs[:2], segment_refs[2:]
    own = row_ref[8:16, : segment_ref.shape[1]]
    targets = square_factor(own)
    sums = 0.0
    for factor_ref, rows_ref in zip(factor_refs, split_refs):
        parts = power_parts(squares(factor_ref[...], targets), 3)
        sums = sums + joined(times(rows_ref[...], parts))
    total = 2 * row_ref.shape[1]
    segment_ref[...] = coil_field(sums, [own[k : k + 1] for k in range(3)], total)


def far_sweep_stage(
    near_row_ref,
    row_ref,
    coil_ref,
    other_ref,
    sums_ref,
    first_ref,
    second_ref,
    out_ref,
    split_ref,
):
    source_rows(row_ref, other_ref[...], split_ref)
    sums = apply(split_ref, [first_ref, second_ref])
    finish(near_row_ref, coil_ref, sums_ref[...] + sums, out_ref)


def near_force_stage(
    row_ref,
    near_source_ref,
    far_source_ref,
    chi_ref,
    field_ref,
    moment_ref,
    sums_ref,
    first_ref,
    second_ref,
    split_ref,
):
    width = chi_ref.shape[1]
    moment_ref[...] = chi_ref[...] * field_ref[:, :width]
    source_rows(row_ref, field_ref[...], split_ref)
    targets = square_factor(row_ref[8:16, :width])
    parts = power_parts(squares(near_source_ref[...], targets), 5)
    sums_ref[...] = joined(times(split_ref[...], parts))
    parts = power_parts(squares(far_source_ref[...], targets), 5)
    first_ref[...] = parts[0]
    second_ref[...] = parts[1]


def far_force_stage(
    near_row_ref,
    row_ref,
    segment_ref,
    other_ref,
    sums_ref,
    first_ref,
    second_ref,
    lorentz_ref,
    split_ref,
):
    width = segment_ref.shape[1]
    source_rows(row_ref, other_ref[...], split_ref)
    sums = sums_ref[...] + joined(times(split_ref[...], [first_ref[...], second_ref[...]]))
    own = near_row_ref[8:16, :width]
    total = 2 * row_ref.shape[1]
    field = segment_ref[...] + dipole_field(sums, [own[k : k + 1] for k in range(3)], total)
    fx, fy, fz = [field[k : k + 1] for k in range(3)]
    cx, cy, cz = [own[3 + k : 4 + k] for k in range(3)]
    lorentz_ref[...] = jnp.concatenate(
        [cy * fz - cz * fy, cz * fx - cx * fz, cx * fy - cy * fx], 0
    )


def call(kernel, outputs, scratch, *operands, limit=VMEM_BYTES, **options):
    return pl.pallas_call(
        kernel,
        out_shape=outputs,
        scratch_shapes=scratch,
        compiler_params=pltpu.CompilerParams(vmem_limit_bytes=limit),
        **options,
    )(*operands)


def close_body(
    seg_mid, seg_vec, strand_of, strand_current, yoke_pos, quad_weight, panel_of, panel_chi
):
    width = yoke_pos.shape[1]
    blocks = lax.axis_size("seg") * lax.axis_size("yoke")
    total = blocks * width
    half = total // 2
    f32, bf16 = jnp.float32, jnp.bfloat16

    def shape(*dims, kind=f32):
        return jax.ShapeDtypeStruct(dims, kind)

    def swap(field):
        return lax.ppermute(field, "yoke", [(0, 1), (1, 0)])

    arrays = [
        seg_mid,
        seg_vec,
        strand_of[None],
        strand_current[None],
        yoke_pos,
        quad_weight[None],
        panel_of[None],
        panel_chi[None],
    ]
    arrays = [pltpu.with_memory_space_constraint(each, pltpu.HBM) for each in arrays]
    packed, chi = call(
        pack_kernel,
        (shape(1, 1, 10 * width), shape(1, width)),
        [pltpu.VMEM(each.shape, each.dtype) for each in arrays]
        + [pltpu.SemaphoreType.DMA((len(arrays),))],
        *arrays,
        in_specs=[pl.BlockSpec(memory_space=pltpu.HBM)] * len(arrays),
    )

    def cross(value, flip):
        return lax.ppermute(value, "seg", [(k, k ^ flip) for k in range(blocks // 2)])

    pair = call(join_kernel, shape(2, 1, 10 * width), [], packed, cross(packed, 4))
    near = call(
        join_kernel,
        shape(8, 1, 10 * width),
        [],
        pair,
        *[cross(pair, flip) for flip in (1, 2, 3)],
    )
    far = swap(near)
    split_scratch = [pltpu.VMEM((48, half), bf16)]
    weight_scratch = [pltpu.VMEM((512, half), bf16)] * 2
    factor = shape(half, 64, kind=bf16)
    split = shape(48, half, kind=bf16)
    matrix = shape(half, half, kind=bf16)
    narrow = shape(half, width, kind=bf16)
    sums, field, row = shape(16, half), shape(3, half), shape(16, half)
    near_row, shift, near_segments, near_sources, targets, near_split, near_sums = call(
        near_coil_stage,
        (row, shape(8, 128), factor, factor, shape(64, half, kind=bf16), split, sums),
        weight_scratch,
        near,
    )
    far_row, far_segments, far_sources, far_split, coil = call(
        far_coil_stage,
        (row, factor, factor, split, field),
        weight_scratch,
        far,
        near_row,
        shift,
        targets,
        near_sums,
    )
    other = swap(coil)
    near_sums, *near_parts = call(
        near_build_stage,
        (sums, matrix, matrix),
        split_scratch,
        near_row,
        near_sources,
        targets,
        coil,
    )
    own, *far_parts = call(
        far_build_stage,
        (field, matrix, matrix),
        split_scratch,
        near_row,
        far_row,
        far_sources,
        targets,
        coil,
        other,
        near_sums,
    )
    for sweep in range(1, ITERS):
        other = swap(own)
        near_sums, segments = call(
            near_sweep_stage,
            (sums, shape(3, width)),
            split_scratch,
            near_row,
            own,
            *near_parts,
            near_segments,
            far_segments,
            near_split,
            far_split,
        )
        own = call(
            far_sweep_stage,
            field,
            split_scratch,
            near_row,
            far_row,
            coil,
            other,
            near_sums,
            *far_parts,
        )
    other = swap(own)
    moment, near_sums, *narrow_parts = call(
        near_force_stage,
        (shape(3, width), shape(16, width), narrow, narrow),
        split_scratch,
        near_row,
        near_sources,
        far_sources,
        chi,
        own,
    )
    lorentz = call(
        far_force_stage,
        shape(3, width),
        split_scratch,
        near_row,
        far_row,
        segments,
        other,
        near_sums,
        *narrow_parts,
    )
    return lorentz, moment


def body(*arrays):
    seg_len, yoke_len = arrays[0].shape[1], arrays[4].shape[1]
    blocks = lax.axis_size("seg") * lax.axis_size("yoke")
    close = seg_len == 256 and yoke_len == 128 and lax.axis_size("yoke") == 2 and blocks == 16
    return (close_body if close else far_body)(*arrays)


def solution(mesh):
    placed = (
        P(None, ("grp", "seg")),
        P(None, ("grp", "seg")),
        P(("grp", "seg")),
        P("grp"),
        P(None, ("grp", "seg", "yoke")),
        P(("grp", "seg", "yoke")),
        P(("grp", "seg", "yoke")),
        P("grp"),
    )
    return jax.shard_map(
        body,
        mesh=mesh,
        in_specs=placed,
        out_specs=(P(None, ("grp", "seg", "yoke")), P(None, ("grp", "seg", "yoke"))),
        check_vma=False,
    )
```

```python
import math

import jax
import jax.numpy as jnp
from jax import lax
from jax.experimental import pallas as pl
from jax.experimental.pallas import tpu as pltpu
from jax.sharding import PartitionSpec as P

ITERS = 2
VMEM_BYTES = 16 << 20


coil_core = 0.05
yoke_core = 0.2


def coil_kernel(targets, sources):
    delta_x = targets[0][:, None] - sources[0][None, :]
    delta_y = targets[1][:, None] - sources[1][None, :]
    delta_z = targets[2][:, None] - sources[2][None, :]
    radial = delta_x * delta_x + delta_y * delta_y + delta_z * delta_z + coil_core * coil_core
    inverse = lax.rsqrt(radial)
    weight_cube = inverse * inverse * inverse
    field_x = jnp.sum(
        weight_cube * (sources[4][None, :] * delta_z - sources[5][None, :] * delta_y), axis=1
    )
    field_y = jnp.sum(
        weight_cube * (sources[5][None, :] * delta_x - sources[3][None, :] * delta_z), axis=1
    )
    field_z = jnp.sum(
        weight_cube * (sources[3][None, :] * delta_y - sources[4][None, :] * delta_x), axis=1
    )
    return jnp.stack([field_x, field_y, field_z], 0)


def dipole_kernel(targets, sources):
    delta_x = targets[0][:, None] - sources[0][None, :]
    delta_y = targets[1][:, None] - sources[1][None, :]
    delta_z = targets[2][:, None] - sources[2][None, :]
    radial = delta_x * delta_x + delta_y * delta_y + delta_z * delta_z
    inverse = lax.rsqrt(radial + yoke_core * yoke_core)
    fifth = inverse * inverse * inverse * inverse * inverse
    along = (
        delta_x * sources[3][None, :]
        + delta_y * sources[4][None, :]
        + delta_z * sources[5][None, :]
    )
    field_x = jnp.sum(fifth * (3.0 * delta_x * along - radial * sources[3][None, :]), axis=1)
    field_y = jnp.sum(fifth * (3.0 * delta_y * along - radial * sources[4][None, :]), axis=1)
    field_z = jnp.sum(fifth * (3.0 * delta_z * along - radial * sources[5][None, :]), axis=1)
    return jnp.stack([field_x, field_y, field_z], 0)


def blocked(kernel, targets, sources, element_limit):
    columns = targets.shape[1]
    pieces = 1
    while pieces < columns and (
        columns % pieces != 0 or columns // pieces * sources.shape[1] > element_limit
    ):
        pieces += 1
    if pieces == 1:
        return kernel(targets, sources)
    stacked = jnp.moveaxis(targets.reshape(3, pieces, columns // pieces), 1, 0)

    def one_block(target_block):
        return kernel(target_block, sources)

    result = lax.map(one_block, stacked)
    return jnp.moveaxis(result, 0, 1).reshape(3, columns)


def fold_blocks(kernel, targets, sources, shard_len):
    columns = sources.shape[1]
    shards = columns // shard_len
    group_size = max(1, (1 << 20) // (targets.shape[1] * shard_len))
    group_size = min(group_size, shards)
    while shards % group_size != 0:
        group_size -= 1
    block_width = group_size * shard_len
    block_count = columns // block_width
    if block_count == 1:
        return kernel(targets, sources)
    stacked = jnp.moveaxis(sources.reshape(sources.shape[0], block_count, block_width), 1, 0)

    def advance(running, source_block):
        return (running + kernel(targets, source_block), None)

    result, unused = lax.scan(advance, jnp.zeros((3, targets.shape[1]), jnp.float32), stacked)
    return result


def make_fold(kernel, targets, shard_len, sources):
    return fold_blocks(kernel, targets, sources, shard_len)


def cross_rows(left_rows, right_rows):
    return jnp.stack(
        [
            left_rows[1] * right_rows[2] - left_rows[2] * right_rows[1],
            left_rows[2] * right_rows[0] - left_rows[0] * right_rows[2],
            left_rows[0] * right_rows[1] - left_rows[1] * right_rows[0],
        ],
        0,
    )


def table_lookup(indices, table):
    rows_iota = lax.broadcasted_iota(jnp.int32, (table.shape[0], indices.shape[0]), 0)
    return jnp.sum(jnp.where(indices[None, :] == rows_iota, table[:, None], 0.0), axis=0)


def far_body(seg_mid, seg_vec, strand_of, strand_current, yoke_pos, quad_weight, panel_of, panel_chi):
    seg_len = seg_mid.shape[1]
    half_len = seg_len // 2
    yoke_len = yoke_pos.shape[1]
    segments_total = seg_len * lax.axis_size("seg")
    points_total = yoke_len * lax.axis_size("seg") * lax.axis_size("yoke")
    coil_scale = 1.0 / math.sqrt(segments_total)
    yoke_scale = 1.0 / math.sqrt(points_total)
    current = table_lookup(strand_of, strand_current)
    carried = current[None, :] * seg_vec
    seg_pack = jnp.concatenate([seg_mid, carried], 0)
    suscept = table_lookup(panel_of, panel_chi)[None, :]
    half_start = lax.axis_index("yoke") * half_len
    own_mid = lax.dynamic_slice_in_dim(seg_mid, half_start, half_len, 1)
    own_carried = lax.dynamic_slice_in_dim(carried, half_start, half_len, 1)
    half_points = lax.all_gather(yoke_pos, "seg", axis=1, tiled=True)
    partial_value = blocked(coil_kernel, half_points, seg_pack, 1 << 19)
    coil_yoke = lax.psum_scatter(partial_value, "seg", scatter_dimension=1, tiled=True) * coil_scale
    coil_seg = (
        make_fold(
            coil_kernel, own_mid, seg_len, lax.all_gather(seg_pack, "seg", axis=1, tiled=True)
        )
        * coil_scale
    )

    def moment_field(targets, moment):
        source_pack = jnp.concatenate([yoke_pos, quad_weight[None, :] * moment], 0)
        gathered_sum = make_fold(
            dipole_kernel,
            targets,
            yoke_len,
            lax.all_gather(source_pack, ("seg", "yoke"), axis=1, tiled=True),
        )
        return gathered_sum * yoke_scale

    moment = suscept * coil_yoke
    for sweep_index in range(ITERS):
        moment = suscept * (coil_yoke + moment_field(yoke_pos, moment))
    total_field = coil_seg + moment_field(own_mid, moment)
    lorentz = cross_rows(own_carried, total_field)
    return (lorentz, moment)


def bf16_parts(value, count):
    parts = []
    for place in range(count):
        part = value.astype(jnp.bfloat16)
        parts.append(part)
        if place + 1 < count:
            value = value - part.astype(jnp.float32)
    return parts


def split_rows(rows, split_ref):
    count = rows.shape[0]
    for place, part in enumerate(bf16_parts(rows, 3)):
        split_ref[place * count : (place + 1) * count, :] = part


def joined(product):
    count = product.shape[0] // 3
    return product[:count] + product[count : 2 * count] + product[2 * count :]


def pick(table_ref, index):
    entries = lax.broadcasted_iota(jnp.int32, (table_ref.shape[1], index.shape[1]), 0)
    chosen = jnp.where(entries == index, 1.0, 0.0).astype(jnp.bfloat16)
    parts = [part.astype(jnp.float32) for part in bf16_parts(table_ref[...], 3)]
    blank = jnp.zeros((5, table_ref.shape[1]), jnp.float32)
    table = jnp.concatenate(parts + [blank], 0).astype(jnp.bfloat16)
    found = jnp.dot(table, chosen, preferred_element_type=jnp.float32)
    return found[0:1] + found[1:2] + found[2:3]


def pack_kernel(*refs):
    sources, (out_ref, chi_ref), held, sems = refs[:8], refs[8:10], refs[10:18], refs[18]
    copies = [
        pltpu.make_async_copy(source, target, sems.at[place])
        for place, (source, target) in enumerate(zip(sources, held))
    ]
    for copy in copies:
        copy.start()
    for copy in copies:
        copy.wait()
    mid_ref, vec_ref, strand_ref, current_ref, pos_ref, weight_ref, panel_ref, table_ref = held
    half = pos_ref.shape[1]
    first = lax.axis_index("yoke") == 0

    def own(ref):
        return jnp.where(first, ref[:, :half], ref[:, half:])

    mid = own(mid_ref)
    carried = pick(current_ref, own(strand_ref)) * own(vec_ref)
    suscept = pick(table_ref, panel_ref[...])
    chi_ref[...] = suscept
    rows = [pos_ref[k : k + 1, :] for k in range(3)]
    rows += [weight_ref[...] * suscept]
    rows += [mid[k : k + 1] for k in range(3)]
    rows += [carried[k : k + 1] for k in range(3)]
    for place, row in enumerate(rows):
        out_ref[0, :, place * half : (place + 1) * half] = row


def join_kernel(*refs):
    place = 0
    for ref in refs[:-1]:
        for block in range(ref.shape[0]):
            refs[-1][place] = ref[block]
            place += 1


def times(rows, matrix_parts, transposed=False):
    contracted = ((1,), (1 if transposed else 0,))
    total = None
    for part in matrix_parts:
        product = lax.dot_general(
            rows, part, (contracted, ((), ())), preferred_element_type=jnp.float32
        )
        total = product if total is None else total + product
    return total


def square_factor(tile, core=None):
    place = lax.broadcasted_iota(jnp.int32, tile.shape, 0)
    points = jnp.where(place < 3, tile, 0.0)
    high, mid, low = [part.astype(jnp.float32) for part in bf16_parts(points, 3)]
    norm = jnp.sum(points * points, axis=0, keepdims=True)
    if core is not None:
        norm = norm + core * core
    norms = [part.astype(jnp.float32) for part in bf16_parts(norm, 3)]
    first = 0 if core is None else 3
    last = jnp.where(place < 6, 1.0, 0.0)
    for k in range(3):
        last = jnp.where(place == first + k, norms[k], last)
    if core is None:
        high, mid, low = -2.0 * high, -2.0 * mid, -2.0 * low
        groups = [high, mid, high, mid, low, high]
    else:
        groups = [high, high, mid, mid, high, low]
    groups += [last, jnp.zeros_like(last)]
    return jnp.concatenate(groups, 0).astype(jnp.bfloat16)


def source_factor(tile, core, out_ref):
    for start in range(0, tile.shape[1], 128):
        factor = square_factor(tile[:, start : start + 128], core)
        out_ref[start : start + 128, :] = factor.T


def power_parts(square, power):
    inverse = lax.rsqrt(square)
    below = inverse * inverse
    return bf16_parts(below * inverse if power == 3 else below * below * inverse, 2)


def squares(sources, targets):
    return jnp.dot(sources, targets, preferred_element_type=jnp.float32)


def coil_rows(segments):
    mx, my, mz, cx, cy, cz = [segments[k : k + 1] for k in range(6)]
    blank = jnp.zeros((10, segments.shape[1]), jnp.float32)
    crossed = [cy * mz - cz * my, cz * mx - cx * mz, cx * my - cy * mx]
    return jnp.concatenate([cx, cy, cz] + crossed + [blank], 0)


def coil_field(sums, targets, total):
    tx, ty, tz = targets
    sx, sy, sz = [sums[k : k + 1] for k in range(3)]
    field = jnp.concatenate([sy * tz - sz * ty, sz * tx - sx * tz, sx * ty - sy * tx], 0)
    return (field - sums[3:6]) * (1.0 / math.sqrt(total))


def place_rows(gathered_ref, row_ref):
    blocks, half = gathered_ref.shape[0], row_ref.shape[1]
    width = half // blocks
    row_ref[...] = jnp.zeros_like(row_ref)
    for block in range(blocks):
        for k in range(10):
            row = k if k < 4 else k + 4
            row_ref[row : row + 1, block * width : (block + 1) * width] = gathered_ref[
                block, :, k * width : (k + 1) * width
            ]


def build_and_apply(factor_ref, targets, power, split_ref, part_refs=()):
    depth, across = 256, 256
    products = []
    for left in range(0, targets.shape[1], across):
        lanes = slice(left, left + across)
        product = None
        for start in range(0, factor_ref.shape[0], depth):
            at = slice(start, start + depth)
            parts = power_parts(squares(factor_ref[at, :], targets[:, lanes]), power)
            for ref, part in zip(part_refs, parts):
                ref[at, lanes] = part
            fresh = times(split_ref[:, at], parts)
            product = fresh if product is None else product + fresh
        products.append(joined(product))
    return jnp.concatenate(products, 1)


def apply(split_ref, part_refs):
    depth = 256
    product = jnp.zeros((split_ref.shape[0], part_refs[0].shape[1]), jnp.float32)
    for start in range(0, split_ref.shape[1], depth):
        rows = split_ref[:, start : start + depth]
        product = product + times(rows, [ref[start : start + depth, :] for ref in part_refs])
    return joined(product)


def near_coil_stage(
    gathered_ref,
    row_ref,
    shift_ref,
    segment_factor_ref,
    yoke_factor_ref,
    target_factor_ref,
    split_ref,
    sums_ref,
):
    half = row_ref.shape[1]
    place_rows(gathered_ref, row_ref)
    center = jnp.sum(row_ref[0:3, :], axis=1, keepdims=True) * (1.0 / half)
    shift = jnp.concatenate([center, jnp.zeros((5, 1), jnp.float32)], 0)
    shift_ref[...] = jnp.broadcast_to(shift, shift_ref.shape)
    yoke = row_ref[0:8, :] - shift
    segments = row_ref[8:16, :] - shift
    row_ref[0:8, :] = yoke
    row_ref[8:16, :] = segments
    target_factor_ref[...] = square_factor(yoke)
    source_factor(segments, coil_core, segment_factor_ref)
    split_rows(coil_rows(segments), split_ref)
    targets = target_factor_ref[...]
    sums_ref[...] = build_and_apply(segment_factor_ref, targets, 3, split_ref)
    source_factor(yoke, yoke_core, yoke_factor_ref)


def far_coil_stage(
    gathered_ref,
    near_row_ref,
    shift_ref,
    target_factor_ref,
    sums_ref,
    row_ref,
    segment_factor_ref,
    yoke_factor_ref,
    split_ref,
    field_ref,
):
    half = row_ref.shape[1]
    place_rows(gathered_ref, row_ref)
    shift = shift_ref[:, 0:1]
    yoke = row_ref[0:8, :] - shift
    segments = row_ref[8:16, :] - shift
    row_ref[0:8, :] = yoke
    row_ref[8:16, :] = segments
    source_factor(segments, coil_core, segment_factor_ref)
    split_rows(coil_rows(segments), split_ref)
    targets = target_factor_ref[...]
    sums = build_and_apply(segment_factor_ref, targets, 3, split_ref)
    places = [near_row_ref[k : k + 1, :] for k in range(3)]
    field_ref[...] = coil_field(sums_ref[...] + sums, places, 2 * half)
    source_factor(yoke, yoke_core, yoke_factor_ref)


def source_rows(row_ref, field, split_ref):
    strength = row_ref[3:4, :] * field
    ux, uy, uz = [strength[k : k + 1] for k in range(3)]
    qx, qy, qz = [row_ref[k : k + 1, :] for k in range(3)]
    along = 3.0 * (qx * ux + qy * uy + qz * uz)
    square = qx * qx + qy * qy + qz * qz
    split_rows(
        jnp.concatenate(
            [
                strength,
                qx * strength,
                qy * strength,
                qz * strength,
                qx * along - square * ux,
                qy * along - square * uy,
                qz * along - square * uz,
                jnp.zeros((1, row_ref.shape[1]), jnp.float32),
            ],
            0,
        ),
        split_ref,
    )


def dipole_field(sums, targets, total):
    tx, ty, tz = targets
    plain = [sums[k : k + 1] for k in range(3)]
    tensor = [[sums[3 + 3 * a + b : 4 + 3 * a + b] for b in range(3)] for a in range(3)]
    toward = tx * plain[0] + ty * plain[1] + tz * plain[2]
    trace = tensor[0][0] + tensor[1][1] + tensor[2][2]
    lead = 3.0 * (toward - trace)
    reach = tx * tx + ty * ty + tz * tz
    fields = []
    for a in range(3):
        field = targets[a] * lead - reach * plain[a] + sums[12 + a : 13 + a]
        for b in range(3):
            field = field + targets[b] * (2.0 * tensor[b][a] - 3.0 * tensor[a][b])
        fields.append(field)
    return jnp.concatenate(fields, 0) * (1.0 / math.sqrt(total))


def near_build_stage(
    row_ref, source_ref, target_ref, field_ref, sums_ref, first_ref, second_ref, split_ref
):
    source_rows(row_ref, field_ref[...], split_ref)
    sums_ref[...] = build_and_apply(
        source_ref, target_ref[...], 5, split_ref, [first_ref, second_ref]
    )


def finish(near_row_ref, coil_ref, sums, out_ref):
    targets = [near_row_ref[k : k + 1, :] for k in range(3)]
    total = 2 * near_row_ref.shape[1]
    out_ref[...] = coil_ref[...] + dipole_field(sums, targets, total)


def far_build_stage(
    near_row_ref,
    row_ref,
    source_ref,
    target_ref,
    coil_ref,
    other_ref,
    sums_ref,
    out_ref,
    first_ref,
    second_ref,
    split_ref,
):
    source_rows(row_ref, other_ref[...], split_ref)
    sums = build_and_apply(source_ref, target_ref[...], 5, split_ref, [first_ref, second_ref])
    finish(near_row_ref, coil_ref, sums_ref[...] + sums, out_ref)


def near_sweep_stage(row_ref, field_ref, first_ref, second_ref, *refs):
    segment_refs, (sums_ref, segment_ref, split_ref) = refs[:-3], refs[-3:]
    source_rows(row_ref, field_ref[...], split_ref)
    sums_ref[...] = apply(split_ref, [first_ref, second_ref])
    factor_refs, split_refs = segment_refs[:2], segment_refs[2:]
    own = row_ref[8:16, : segment_ref.shape[1]]
    targets = square_factor(own)
    sums = 0.0
    for factor_ref, rows_ref in zip(factor_refs, split_refs):
        parts = power_parts(squares(factor_ref[...], targets), 3)
        sums = sums + joined(times(rows_ref[...], parts))
    total = 2 * row_ref.shape[1]
    segment_ref[...] = coil_field(sums, [own[k : k + 1] for k in range(3)], total)


def far_sweep_stage(
    near_row_ref,
    row_ref,
    source_ref,
    coil_ref,
    other_ref,
    sums_ref,
    first_ref,
    second_ref,
    out_ref,
    narrow_first_ref,
    narrow_second_ref,
    split_ref,
):
    targets = square_factor(near_row_ref[8:16, : narrow_first_ref.shape[1]])
    parts = power_parts(squares(source_ref[...], targets), 5)
    narrow_first_ref[...] = parts[0]
    narrow_second_ref[...] = parts[1]
    source_rows(row_ref, other_ref[...], split_ref)
    sums = apply(split_ref, [first_ref, second_ref])
    finish(near_row_ref, coil_ref, sums_ref[...] + sums, out_ref)


def near_force_stage(
    row_ref,
    source_ref,
    field_ref,
    sums_ref,
    split_ref,
):
    source_rows(row_ref, field_ref[...], split_ref)
    targets = square_factor(row_ref[8:16, : sums_ref.shape[1]])
    parts = power_parts(squares(source_ref[...], targets), 5)
    sums_ref[...] = joined(times(split_ref[...], parts))


def far_force_stage(
    near_row_ref,
    row_ref,
    segment_ref,
    chi_ref,
    field_ref,
    other_ref,
    sums_ref,
    first_ref,
    second_ref,
    lorentz_ref,
    moment_ref,
    split_ref,
):
    width = segment_ref.shape[1]
    moment_ref[...] = chi_ref[...] * field_ref[:, :width]
    source_rows(row_ref, other_ref[...], split_ref)
    sums = sums_ref[...] + joined(times(split_ref[...], [first_ref[...], second_ref[...]]))
    own = near_row_ref[8:16, :width]
    total = 2 * row_ref.shape[1]
    field = segment_ref[...] + dipole_field(sums, [own[k : k + 1] for k in range(3)], total)
    fx, fy, fz = [field[k : k + 1] for k in range(3)]
    cx, cy, cz = [own[3 + k : 4 + k] for k in range(3)]
    lorentz_ref[...] = jnp.concatenate(
        [cy * fz - cz * fy, cz * fx - cx * fz, cx * fy - cy * fx], 0
    )


def call(kernel, outputs, scratch, *operands, limit=VMEM_BYTES, **options):
    return pl.pallas_call(
        kernel,
        out_shape=outputs,
        scratch_shapes=scratch,
        compiler_params=pltpu.CompilerParams(vmem_limit_bytes=limit),
        **options,
    )(*operands)


def close_body(
    seg_mid, seg_vec, strand_of, strand_current, yoke_pos, quad_weight, panel_of, panel_chi
):
    width = yoke_pos.shape[1]
    blocks = lax.axis_size("seg") * lax.axis_size("yoke")
    total = blocks * width
    half = total // 2
    f32, bf16 = jnp.float32, jnp.bfloat16

    def shape(*dims, kind=f32):
        return jax.ShapeDtypeStruct(dims, kind)

    def swap(field):
        return lax.ppermute(field, "yoke", [(0, 1), (1, 0)])

    arrays = [
        seg_mid,
        seg_vec,
        strand_of[None],
        strand_current[None],
        yoke_pos,
        quad_weight[None],
        panel_of[None],
        panel_chi[None],
    ]
    arrays = [pltpu.with_memory_space_constraint(each, pltpu.HBM) for each in arrays]
    packed, chi = call(
        pack_kernel,
        (shape(1, 1, 10 * width), shape(1, width)),
        [pltpu.VMEM(each.shape, each.dtype) for each in arrays]
        + [pltpu.SemaphoreType.DMA((len(arrays),))],
        *arrays,
        in_specs=[pl.BlockSpec(memory_space=pltpu.HBM)] * len(arrays),
    )

    def cross(value, flip):
        return lax.ppermute(value, "seg", [(k, k ^ flip) for k in range(blocks // 2)])

    pair = call(join_kernel, shape(2, 1, 10 * width), [], packed, cross(packed, 4))
    near = call(
        join_kernel,
        shape(8, 1, 10 * width),
        [],
        pair,
        *[cross(pair, flip) for flip in (1, 2, 3)],
    )
    far = swap(near)
    split_scratch = [pltpu.VMEM((48, half), bf16)]
    factor = shape(half, 64, kind=bf16)
    split = shape(48, half, kind=bf16)
    matrix = shape(half, half, kind=bf16)
    narrow = shape(half, width, kind=bf16)
    sums, field, row = shape(16, half), shape(3, half), shape(16, half)
    near_row, shift, near_segments, near_sources, targets, near_split, near_sums = call(
        near_coil_stage,
        (row, shape(8, 128), factor, factor, shape(64, half, kind=bf16), split, sums),
        [],
        near,
    )
    far_row, far_segments, far_sources, far_split, coil = call(
        far_coil_stage,
        (row, factor, factor, split, field),
        [],
        far,
        near_row,
        shift,
        targets,
        near_sums,
    )
    other = swap(coil)
    near_sums, *near_parts = call(
        near_build_stage,
        (sums, matrix, matrix),
        split_scratch,
        near_row,
        near_sources,
        targets,
        coil,
    )
    own, *far_parts = call(
        far_build_stage,
        (field, matrix, matrix),
        split_scratch,
        near_row,
        far_row,
        far_sources,
        targets,
        coil,
        other,
        near_sums,
    )
    for sweep in range(1, ITERS):
        other = swap(own)
        near_sums, segments = call(
            near_sweep_stage,
            (sums, shape(3, width)),
            split_scratch,
            near_row,
            own,
            *near_parts,
            near_segments,
            far_segments,
            near_split,
            far_split,
        )
        own, *narrow_parts = call(
            far_sweep_stage,
            (field, narrow, narrow),
            split_scratch,
            near_row,
            far_row,
            far_sources,
            coil,
            other,
            near_sums,
            *far_parts,
        )
    other = swap(own)
    near_sums = call(
        near_force_stage,
        shape(16, width),
        split_scratch,
        near_row,
        near_sources,
        own,
    )
    lorentz, moment = call(
        far_force_stage,
        (shape(3, width), shape(3, width)),
        split_scratch,
        near_row,
        far_row,
        segments,
        chi,
        own,
        other,
        near_sums,
        *narrow_parts,
    )
    return lorentz, moment


def body(*arrays):
    seg_len, yoke_len = arrays[0].shape[1], arrays[4].shape[1]
    blocks = lax.axis_size("seg") * lax.axis_size("yoke")
    close = seg_len == 256 and yoke_len == 128 and lax.axis_size("yoke") == 2 and blocks == 16
    return (close_body if close else far_body)(*arrays)


def solution(mesh):
    placed = (
        P(None, ("grp", "seg")),
        P(None, ("grp", "seg")),
        P(("grp", "seg")),
        P("grp"),
        P(None, ("grp", "seg", "yoke")),
        P(("grp", "seg", "yoke")),
        P(("grp", "seg", "yoke")),
        P("grp"),
    )
    return jax.shard_map(
        body,
        mesh=mesh,
        in_specs=placed,
        out_specs=(P(None, ("grp", "seg", "yoke")), P(None, ("grp", "seg", "yoke"))),
        check_vma=False,
    )
```

```python
import math

import jax
import jax.numpy as jnp
from jax import lax
from jax.experimental import pallas as pl
from jax.experimental.pallas import tpu as pltpu
from jax.sharding import PartitionSpec as P

ITERS = 2
VMEM_BYTES = 16 << 20


coil_core = 0.05
yoke_core = 0.2


def coil_kernel(targets, sources):
    delta_x = targets[0][:, None] - sources[0][None, :]
    delta_y = targets[1][:, None] - sources[1][None, :]
    delta_z = targets[2][:, None] - sources[2][None, :]
    radial = delta_x * delta_x + delta_y * delta_y + delta_z * delta_z + coil_core * coil_core
    inverse = lax.rsqrt(radial)
    weight_cube = inverse * inverse * inverse
    field_x = jnp.sum(
        weight_cube * (sources[4][None, :] * delta_z - sources[5][None, :] * delta_y), axis=1
    )
    field_y = jnp.sum(
        weight_cube * (sources[5][None, :] * delta_x - sources[3][None, :] * delta_z), axis=1
    )
    field_z = jnp.sum(
        weight_cube * (sources[3][None, :] * delta_y - sources[4][None, :] * delta_x), axis=1
    )
    return jnp.stack([field_x, field_y, field_z], 0)


def dipole_kernel(targets, sources):
    delta_x = targets[0][:, None] - sources[0][None, :]
    delta_y = targets[1][:, None] - sources[1][None, :]
    delta_z = targets[2][:, None] - sources[2][None, :]
    radial = delta_x * delta_x + delta_y * delta_y + delta_z * delta_z
    inverse = lax.rsqrt(radial + yoke_core * yoke_core)
    fifth = inverse * inverse * inverse * inverse * inverse
    along = (
        delta_x * sources[3][None, :]
        + delta_y * sources[4][None, :]
        + delta_z * sources[5][None, :]
    )
    field_x = jnp.sum(fifth * (3.0 * delta_x * along - radial * sources[3][None, :]), axis=1)
    field_y = jnp.sum(fifth * (3.0 * delta_y * along - radial * sources[4][None, :]), axis=1)
    field_z = jnp.sum(fifth * (3.0 * delta_z * along - radial * sources[5][None, :]), axis=1)
    return jnp.stack([field_x, field_y, field_z], 0)


def blocked(kernel, targets, sources, element_limit):
    columns = targets.shape[1]
    pieces = 1
    while pieces < columns and (
        columns % pieces != 0 or columns // pieces * sources.shape[1] > element_limit
    ):
        pieces += 1
    if pieces == 1:
        return kernel(targets, sources)
    stacked = jnp.moveaxis(targets.reshape(3, pieces, columns // pieces), 1, 0)

    def one_block(target_block):
        return kernel(target_block, sources)

    result = lax.map(one_block, stacked)
    return jnp.moveaxis(result, 0, 1).reshape(3, columns)


def fold_blocks(kernel, targets, sources, shard_len):
    columns = sources.shape[1]
    shards = columns // shard_len
    group_size = max(1, (1 << 20) // (targets.shape[1] * shard_len))
    group_size = min(group_size, shards)
    while shards % group_size != 0:
        group_size -= 1
    block_width = group_size * shard_len
    block_count = columns // block_width
    if block_count == 1:
        return kernel(targets, sources)
    stacked = jnp.moveaxis(sources.reshape(sources.shape[0], block_count, block_width), 1, 0)

    def advance(running, source_block):
        return (running + kernel(targets, source_block), None)

    result, unused = lax.scan(advance, jnp.zeros((3, targets.shape[1]), jnp.float32), stacked)
    return result


def make_fold(kernel, targets, shard_len, sources):
    return fold_blocks(kernel, targets, sources, shard_len)


def cross_rows(left_rows, right_rows):
    return jnp.stack(
        [
            left_rows[1] * right_rows[2] - left_rows[2] * right_rows[1],
            left_rows[2] * right_rows[0] - left_rows[0] * right_rows[2],
            left_rows[0] * right_rows[1] - left_rows[1] * right_rows[0],
        ],
        0,
    )


def table_lookup(indices, table):
    rows_iota = lax.broadcasted_iota(jnp.int32, (table.shape[0], indices.shape[0]), 0)
    return jnp.sum(jnp.where(indices[None, :] == rows_iota, table[:, None], 0.0), axis=0)


def far_body(seg_mid, seg_vec, strand_of, strand_current, yoke_pos, quad_weight, panel_of, panel_chi):
    seg_len = seg_mid.shape[1]
    half_len = seg_len // 2
    yoke_len = yoke_pos.shape[1]
    segments_total = seg_len * lax.axis_size("seg")
    points_total = yoke_len * lax.axis_size("seg") * lax.axis_size("yoke")
    coil_scale = 1.0 / math.sqrt(segments_total)
    yoke_scale = 1.0 / math.sqrt(points_total)
    current = table_lookup(strand_of, strand_current)
    carried = current[None, :] * seg_vec
    seg_pack = jnp.concatenate([seg_mid, carried], 0)
    suscept = table_lookup(panel_of, panel_chi)[None, :]
    half_start = lax.axis_index("yoke") * half_len
    own_mid = lax.dynamic_slice_in_dim(seg_mid, half_start, half_len, 1)
    own_carried = lax.dynamic_slice_in_dim(carried, half_start, half_len, 1)
    half_points = lax.all_gather(yoke_pos, "seg", axis=1, tiled=True)
    partial_value = blocked(coil_kernel, half_points, seg_pack, 1 << 19)
    coil_yoke = lax.psum_scatter(partial_value, "seg", scatter_dimension=1, tiled=True) * coil_scale
    coil_seg = (
        make_fold(
            coil_kernel, own_mid, seg_len, lax.all_gather(seg_pack, "seg", axis=1, tiled=True)
        )
        * coil_scale
    )

    def moment_field(targets, moment):
        source_pack = jnp.concatenate([yoke_pos, quad_weight[None, :] * moment], 0)
        gathered_sum = make_fold(
            dipole_kernel,
            targets,
            yoke_len,
            lax.all_gather(source_pack, ("seg", "yoke"), axis=1, tiled=True),
        )
        return gathered_sum * yoke_scale

    moment = suscept * coil_yoke
    for sweep_index in range(ITERS):
        moment = suscept * (coil_yoke + moment_field(yoke_pos, moment))
    total_field = coil_seg + moment_field(own_mid, moment)
    lorentz = cross_rows(own_carried, total_field)
    return (lorentz, moment)


def bf16_parts(value, count):
    parts = []
    for place in range(count):
        part = value.astype(jnp.bfloat16)
        parts.append(part)
        if place + 1 < count:
            value = value - part.astype(jnp.float32)
    return parts


def split_rows(rows, split_ref):
    count = rows.shape[0]
    parts = bf16_parts(rows, 3)
    if count % 16 == 0:
        for place, part in enumerate(parts):
            split_ref[place * count : (place + 1) * count, :] = part
    else:
        parts = [part.astype(jnp.float32) for part in parts] + [jnp.zeros_like(rows)]
        split_ref[...] = jnp.concatenate(parts, 0).astype(jnp.bfloat16)


def joined(product):
    count = product.shape[0] // 24 * 8
    return product[:count] + product[count : 2 * count] + product[2 * count : 3 * count]


def pick(table_ref, index):
    entries = lax.broadcasted_iota(jnp.int32, (table_ref.shape[1], index.shape[1]), 0)
    chosen = jnp.where(entries == index, 1.0, 0.0).astype(jnp.bfloat16)
    parts = [part.astype(jnp.float32) for part in bf16_parts(table_ref[...], 3)]
    blank = jnp.zeros((5, table_ref.shape[1]), jnp.float32)
    table = jnp.concatenate(parts + [blank], 0).astype(jnp.bfloat16)
    found = jnp.dot(table, chosen, preferred_element_type=jnp.float32)
    return found[0:1] + found[1:2] + found[2:3]


def pack_kernel(*refs):
    sources, (out_ref, chi_ref), held, sems = refs[:8], refs[8:10], refs[10:18], refs[18]
    copies = [
        pltpu.make_async_copy(source, target, sems.at[place])
        for place, (source, target) in enumerate(zip(sources, held))
    ]
    for copy in copies:
        copy.start()
    for copy in copies:
        copy.wait()
    mid_ref, vec_ref, strand_ref, current_ref, pos_ref, weight_ref, panel_ref, table_ref = held
    half = pos_ref.shape[1]
    first = lax.axis_index("yoke") == 0

    def own(ref):
        return jnp.where(first, ref[:, :half], ref[:, half:])

    mid = own(mid_ref)
    carried = pick(current_ref, own(strand_ref)) * own(vec_ref)
    suscept = pick(table_ref, panel_ref[...])
    chi_ref[...] = suscept
    rows = [pos_ref[k : k + 1, :] for k in range(3)]
    rows += [weight_ref[...] * suscept]
    rows += [mid[k : k + 1] for k in range(3)]
    rows += [carried[k : k + 1] for k in range(3)]
    for place, row in enumerate(rows):
        out_ref[0, :, place * half : (place + 1) * half] = row


def join_kernel(*refs):
    place = 0
    for ref in refs[:-1]:
        for block in range(ref.shape[0]):
            refs[-1][place] = ref[block]
            place += 1


def times(rows, matrix_parts, transposed=False):
    contracted = ((1,), (1 if transposed else 0,))
    total = None
    for part in matrix_parts:
        product = lax.dot_general(
            rows, part, (contracted, ((), ())), preferred_element_type=jnp.float32
        )
        total = product if total is None else total + product
    return total


def square_factor(tile, core=None):
    place = lax.broadcasted_iota(jnp.int32, tile.shape, 0)
    points = jnp.where(place < 3, tile, 0.0)
    high, mid, low = [part.astype(jnp.float32) for part in bf16_parts(points, 3)]
    norm = jnp.sum(points * points, axis=0, keepdims=True)
    if core is not None:
        norm = norm + core * core
    norms = [part.astype(jnp.float32) for part in bf16_parts(norm, 3)]
    first = 0 if core is None else 3
    last = jnp.where(place < 6, 1.0, 0.0)
    for k in range(3):
        last = jnp.where(place == first + k, norms[k], last)
    if core is None:
        high, mid, low = -2.0 * high, -2.0 * mid, -2.0 * low
        groups = [high, mid, high, mid, low, high]
    else:
        groups = [high, high, mid, mid, high, low]
    groups += [last, jnp.zeros_like(last)]
    return jnp.concatenate(groups, 0).astype(jnp.bfloat16)


def source_factor(tile, core, out_ref):
    for start in range(0, tile.shape[1], 128):
        factor = square_factor(tile[:, start : start + 128], core)
        out_ref[start : start + 128, :] = factor.T


def power_parts(square, power):
    inverse = lax.rsqrt(square)
    below = inverse * inverse
    return bf16_parts(below * inverse if power == 3 else below * below * inverse, 2)


def squares(sources, targets):
    return jnp.dot(sources, targets, preferred_element_type=jnp.float32)


def coil_rows(segments):
    mx, my, mz, cx, cy, cz = [segments[k : k + 1] for k in range(6)]
    blank = jnp.zeros((2, segments.shape[1]), jnp.float32)
    crossed = [cy * mz - cz * my, cz * mx - cx * mz, cx * my - cy * mx]
    return jnp.concatenate([cx, cy, cz] + crossed + [blank], 0)


def coil_field(sums, targets, total):
    tx, ty, tz = targets
    sx, sy, sz = [sums[k : k + 1] for k in range(3)]
    field = jnp.concatenate([sy * tz - sz * ty, sz * tx - sx * tz, sx * ty - sy * tx], 0)
    return (field - sums[3:6]) * (1.0 / math.sqrt(total))


def place_rows(gathered_ref, row_ref):
    blocks, half = gathered_ref.shape[0], row_ref.shape[1]
    width = half // blocks
    row_ref[...] = jnp.zeros_like(row_ref)
    for block in range(blocks):
        for k in range(10):
            row = k if k < 4 else k + 4
            row_ref[row : row + 1, block * width : (block + 1) * width] = gathered_ref[
                block, :, k * width : (k + 1) * width
            ]


def build_and_apply(factor_ref, targets, power, split_ref, part_refs=()):
    depth, across = 256, 256
    products = []
    for left in range(0, targets.shape[1], across):
        lanes = slice(left, left + across)
        product = None
        for start in range(0, factor_ref.shape[0], depth):
            at = slice(start, start + depth)
            parts = power_parts(squares(factor_ref[at, :], targets[:, lanes]), power)
            for ref, part in zip(part_refs, parts):
                ref[at, lanes] = part
            fresh = times(split_ref[:, at], parts)
            product = fresh if product is None else product + fresh
        products.append(joined(product))
    return jnp.concatenate(products, 1)


def apply(split_ref, part_refs):
    depth = 256
    product = jnp.zeros((split_ref.shape[0], part_refs[0].shape[1]), jnp.float32)
    for start in range(0, split_ref.shape[1], depth):
        rows = split_ref[:, start : start + depth]
        product = product + times(rows, [ref[start : start + depth, :] for ref in part_refs])
    return joined(product)


def near_coil_stage(
    gathered_ref,
    row_ref,
    shift_ref,
    segment_factor_ref,
    yoke_factor_ref,
    target_factor_ref,
    split_ref,
    sums_ref,
):
    half = row_ref.shape[1]
    place_rows(gathered_ref, row_ref)
    center = jnp.sum(row_ref[0:3, :], axis=1, keepdims=True) * (1.0 / half)
    shift = jnp.concatenate([center, jnp.zeros((5, 1), jnp.float32)], 0)
    shift_ref[...] = jnp.broadcast_to(shift, shift_ref.shape)
    yoke = row_ref[0:8, :] - shift
    segments = row_ref[8:16, :] - shift
    row_ref[0:8, :] = yoke
    row_ref[8:16, :] = segments
    target_factor_ref[...] = square_factor(yoke)
    source_factor(segments, coil_core, segment_factor_ref)
    split_rows(coil_rows(segments), split_ref)
    targets = target_factor_ref[...]
    sums_ref[...] = build_and_apply(segment_factor_ref, targets, 3, split_ref)
    source_factor(yoke, yoke_core, yoke_factor_ref)


def far_coil_stage(
    gathered_ref,
    near_row_ref,
    shift_ref,
    target_factor_ref,
    sums_ref,
    row_ref,
    segment_factor_ref,
    yoke_factor_ref,
    split_ref,
    field_ref,
):
    half = row_ref.shape[1]
    place_rows(gathered_ref, row_ref)
    shift = shift_ref[:, 0:1]
    yoke = row_ref[0:8, :] - shift
    segments = row_ref[8:16, :] - shift
    row_ref[0:8, :] = yoke
    row_ref[8:16, :] = segments
    source_factor(segments, coil_core, segment_factor_ref)
    split_rows(coil_rows(segments), split_ref)
    targets = target_factor_ref[...]
    sums = build_and_apply(segment_factor_ref, targets, 3, split_ref)
    places = [near_row_ref[k : k + 1, :] for k in range(3)]
    field_ref[...] = coil_field(sums_ref[...] + sums, places, 2 * half)
    source_factor(yoke, yoke_core, yoke_factor_ref)


def source_rows(row_ref, field, split_ref):
    strength = row_ref[3:4, :] * field
    ux, uy, uz = [strength[k : k + 1] for k in range(3)]
    qx, qy, qz = [row_ref[k : k + 1, :] for k in range(3)]
    along = 3.0 * (qx * ux + qy * uy + qz * uz)
    square = qx * qx + qy * qy + qz * qz
    split_rows(
        jnp.concatenate(
            [
                strength,
                qx * strength,
                qy * strength,
                qz * strength,
                qx * along - square * ux,
                qy * along - square * uy,
                qz * along - square * uz,
                jnp.zeros((1, row_ref.shape[1]), jnp.float32),
            ],
            0,
        ),
        split_ref,
    )


def dipole_field(sums, targets, total):
    tx, ty, tz = targets
    plain = [sums[k : k + 1] for k in range(3)]
    tensor = [[sums[3 + 3 * a + b : 4 + 3 * a + b] for b in range(3)] for a in range(3)]
    toward = tx * plain[0] + ty * plain[1] + tz * plain[2]
    trace = tensor[0][0] + tensor[1][1] + tensor[2][2]
    lead = 3.0 * (toward - trace)
    reach = tx * tx + ty * ty + tz * tz
    fields = []
    for a in range(3):
        field = targets[a] * lead - reach * plain[a] + sums[12 + a : 13 + a]
        for b in range(3):
            field = field + targets[b] * (2.0 * tensor[b][a] - 3.0 * tensor[a][b])
        fields.append(field)
    return jnp.concatenate(fields, 0) * (1.0 / math.sqrt(total))


def near_build_stage(
    row_ref, source_ref, target_ref, field_ref, sums_ref, first_ref, second_ref, split_ref
):
    source_rows(row_ref, field_ref[...], split_ref)
    sums_ref[...] = build_and_apply(
        source_ref, target_ref[...], 5, split_ref, [first_ref, second_ref]
    )


def finish(near_row_ref, coil_ref, sums, out_ref):
    targets = [near_row_ref[k : k + 1, :] for k in range(3)]
    total = 2 * near_row_ref.shape[1]
    out_ref[...] = coil_ref[...] + dipole_field(sums, targets, total)


def far_build_stage(
    near_row_ref,
    row_ref,
    source_ref,
    target_ref,
    coil_ref,
    other_ref,
    sums_ref,
    out_ref,
    first_ref,
    second_ref,
    split_ref,
):
    source_rows(row_ref, other_ref[...], split_ref)
    sums = build_and_apply(source_ref, target_ref[...], 5, split_ref, [first_ref, second_ref])
    finish(near_row_ref, coil_ref, sums_ref[...] + sums, out_ref)


def segment_sums(row_ref, factor_ref, rows_ref, width):
    targets = square_factor(row_ref[8:16, :width])
    parts = power_parts(squares(factor_ref[...], targets), 3)
    return joined(times(rows_ref[...], parts))


def near_sweep_stage(
    row_ref,
    field_ref,
    first_ref,
    second_ref,
    factor_ref,
    rows_ref,
    sums_ref,
    segment_sums_ref,
    split_ref,
):
    source_rows(row_ref, field_ref[...], split_ref)
    sums_ref[...] = apply(split_ref, [first_ref, second_ref])
    width = segment_sums_ref.shape[1]
    segment_sums_ref[...] = segment_sums(row_ref, factor_ref, rows_ref, width)


def far_sweep_stage(
    near_row_ref,
    row_ref,
    source_ref,
    coil_ref,
    other_ref,
    sums_ref,
    first_ref,
    second_ref,
    out_ref,
    narrow_first_ref,
    narrow_second_ref,
    split_ref,
):
    targets = square_factor(near_row_ref[8:16, : narrow_first_ref.shape[1]])
    parts = power_parts(squares(source_ref[...], targets), 5)
    narrow_first_ref[...] = parts[0]
    narrow_second_ref[...] = parts[1]
    source_rows(row_ref, other_ref[...], split_ref)
    sums = apply(split_ref, [first_ref, second_ref])
    finish(near_row_ref, coil_ref, sums_ref[...] + sums, out_ref)


def near_force_stage(
    row_ref,
    source_ref,
    field_ref,
    factor_ref,
    rows_ref,
    segment_sums_ref,
    sums_ref,
    segment_ref,
    split_ref,
):
    source_rows(row_ref, field_ref[...], split_ref)
    width = sums_ref.shape[1]
    own = row_ref[8:16, :width]
    parts = power_parts(squares(source_ref[...], square_factor(own)), 5)
    sums_ref[...] = joined(times(split_ref[...], parts))
    sums = segment_sums_ref[...] + segment_sums(row_ref, factor_ref, rows_ref, width)
    total = 2 * row_ref.shape[1]
    segment_ref[...] = coil_field(sums, [own[k : k + 1] for k in range(3)], total)


def far_force_stage(
    near_row_ref,
    row_ref,
    segment_ref,
    chi_ref,
    field_ref,
    other_ref,
    sums_ref,
    first_ref,
    second_ref,
    lorentz_ref,
    moment_ref,
    split_ref,
):
    width = segment_ref.shape[1]
    moment_ref[...] = chi_ref[...] * field_ref[:, :width]
    source_rows(row_ref, other_ref[...], split_ref)
    sums = sums_ref[...] + joined(times(split_ref[...], [first_ref[...], second_ref[...]]))
    own = near_row_ref[8:16, :width]
    total = 2 * row_ref.shape[1]
    field = segment_ref[...] + dipole_field(sums, [own[k : k + 1] for k in range(3)], total)
    fx, fy, fz = [field[k : k + 1] for k in range(3)]
    cx, cy, cz = [own[3 + k : 4 + k] for k in range(3)]
    lorentz_ref[...] = jnp.concatenate(
        [cy * fz - cz * fy, cz * fx - cx * fz, cx * fy - cy * fx], 0
    )


def call(kernel, outputs, scratch, *operands, limit=VMEM_BYTES, **options):
    return pl.pallas_call(
        kernel,
        out_shape=outputs,
        scratch_shapes=scratch,
        compiler_params=pltpu.CompilerParams(vmem_limit_bytes=limit),
        **options,
    )(*operands)


def close_body(
    seg_mid, seg_vec, strand_of, strand_current, yoke_pos, quad_weight, panel_of, panel_chi
):
    width = yoke_pos.shape[1]
    blocks = lax.axis_size("seg") * lax.axis_size("yoke")
    total = blocks * width
    half = total // 2
    f32, bf16 = jnp.float32, jnp.bfloat16

    def shape(*dims, kind=f32):
        return jax.ShapeDtypeStruct(dims, kind)

    def swap(field):
        return lax.ppermute(field, "yoke", [(0, 1), (1, 0)])

    arrays = [
        seg_mid,
        seg_vec,
        strand_of[None],
        strand_current[None],
        yoke_pos,
        quad_weight[None],
        panel_of[None],
        panel_chi[None],
    ]
    arrays = [pltpu.with_memory_space_constraint(each, pltpu.HBM) for each in arrays]
    packed, chi = call(
        pack_kernel,
        (shape(1, 1, 10 * width), shape(1, width)),
        [pltpu.VMEM(each.shape, each.dtype) for each in arrays]
        + [pltpu.SemaphoreType.DMA((len(arrays),))],
        *arrays,
        in_specs=[pl.BlockSpec(memory_space=pltpu.HBM)] * len(arrays),
    )

    def cross(value, flip):
        return lax.ppermute(value, "seg", [(k, k ^ flip) for k in range(blocks // 2)])

    pair = call(join_kernel, shape(2, 1, 10 * width), [], packed, cross(packed, 4))
    near = call(
        join_kernel,
        shape(8, 1, 10 * width),
        [],
        pair,
        *[cross(pair, flip) for flip in (1, 2, 3)],
    )
    far = swap(near)
    split_scratch = [pltpu.VMEM((48, half), bf16)]
    factor = shape(half, 64, kind=bf16)
    split = shape(32, half, kind=bf16)
    matrix = shape(half, half, kind=bf16)
    narrow = shape(half, width, kind=bf16)
    sums, field, row = shape(16, half), shape(3, half), shape(16, half)
    near_row, shift, near_segments, near_sources, targets, near_split, near_sums = call(
        near_coil_stage,
        (row, shape(8, 128), factor, factor, shape(64, half, kind=bf16), split, shape(8, half)),
        [],
        near,
    )
    far_row, far_segments, far_sources, far_split, coil = call(
        far_coil_stage,
        (row, factor, factor, split, field),
        [],
        far,
        near_row,
        shift,
        targets,
        near_sums,
    )
    other = swap(coil)
    near_sums, *near_parts = call(
        near_build_stage,
        (sums, matrix, matrix),
        split_scratch,
        near_row,
        near_sources,
        targets,
        coil,
    )
    own, *far_parts = call(
        far_build_stage,
        (field, matrix, matrix),
        split_scratch,
        near_row,
        far_row,
        far_sources,
        targets,
        coil,
        other,
        near_sums,
    )
    for sweep in range(1, ITERS):
        other = swap(own)
        near_sums, segment_part = call(
            near_sweep_stage,
            (sums, shape(8, width)),
            split_scratch,
            near_row,
            own,
            *near_parts,
            near_segments,
            near_split,
        )
        own, *narrow_parts = call(
            far_sweep_stage,
            (field, narrow, narrow),
            split_scratch,
            near_row,
            far_row,
            far_sources,
            coil,
            other,
            near_sums,
            *far_parts,
        )
    other = swap(own)
    near_sums, segments = call(
        near_force_stage,
        (shape(16, width), shape(3, width)),
        split_scratch,
        near_row,
        near_sources,
        own,
        far_segments,
        far_split,
        segment_part,
    )
    lorentz, moment = call(
        far_force_stage,
        (shape(3, width), shape(3, width)),
        split_scratch,
        near_row,
        far_row,
        segments,
        chi,
        own,
        other,
        near_sums,
        *narrow_parts,
    )
    return lorentz, moment


def body(*arrays):
    seg_len, yoke_len = arrays[0].shape[1], arrays[4].shape[1]
    blocks = lax.axis_size("seg") * lax.axis_size("yoke")
    close = seg_len == 256 and yoke_len == 128 and lax.axis_size("yoke") == 2 and blocks == 16
    return (close_body if close else far_body)(*arrays)


def solution(mesh):
    placed = (
        P(None, ("grp", "seg")),
        P(None, ("grp", "seg")),
        P(("grp", "seg")),
        P("grp"),
        P(None, ("grp", "seg", "yoke")),
        P(("grp", "seg", "yoke")),
        P(("grp", "seg", "yoke")),
        P("grp"),
    )
    return jax.shard_map(
        body,
        mesh=mesh,
        in_specs=placed,
        out_specs=(P(None, ("grp", "seg", "yoke")), P(None, ("grp", "seg", "yoke"))),
        check_vma=False,
    )
```
